32 devices in a mesh: front: 4 (over z), row: 4 (over y, x), col: 2 (over core).
Axes of the slice: x: 2, y: 2, z: 4, core: 2. Of those that a mesh axis runs over, the one named last changes fastest.
Arguments:
- front_matrix: float32 [4, 24, 512, 3072], P('front', None, 'row', 'col')
- front_sizes: int32 [4], P('front'), may hold values from 8192 to 12288, as said below
- contrib: float32 [4, 4, 512, 3072], P('front', None, 'row', 'col'), may hold values from -6 to 6
- dest_front: int32 [4, 4, 4], P('front', None, 'row'), may hold values from 0 to 3, as said below
- dest_local: int32 [4, 4, 4], P('front', None, 'row'), may hold values from 2 to 23, as said below
Outputs:
- factored: float32 [4, 24, 512, 3072], P('front', None, 'row', 'col')
The draws below stay inside these ranges and needn't reach their ends.
Inputs may be any that keep to these rules, and one draw needn't show every extreme that they name: `front_sizes`: multiples of 128; every draw has a front of order 12288 and one of order 8192. For each (g, r), the 4 entries dest_front[g, :, r] name distinct fronts. The block (g, k, r) lands on parent rows from (dest_local * 4 + r) * 128: at or after row 1024 and wholly below the parent's order; several blocks may land on the same rows; in every draw some block lands in the last round of blocks of the largest front.
All inputs are finite; a program needn't handle non-finite values.
Results may differ from the reference program's by a relative error of at most 0.0003.
Values sent between devices are 32-bit elements; how exact they have to be, the bound alone decides.
No kernel may reach another device: no remote copies, remote signals or barrier semaphores. Data moves between devices by JAX's collectives and lax.ppermute only.
A program may use at most 128 MiB of HBM per device.

```python
import jax
import jax.numpy as jnp
from jax import lax

FMAX = 12288
FMIN = 8192
PW = 512
BLK = 128
NPANEL = 2
KB = 4
FRONTS = 4
CYCLE = 512
LOCB = 24
W = 3072


def rank_of_fronts(key):
    size_key = jax.random.fold_in(key, 7)
    first_key, rank_key = jax.random.split(size_key)
    return (first_key, jax.random.permutation(rank_key, FRONTS))


def layout_sizes(key):
    first_key, rank_order = rank_of_fronts(key)
    steps_count = (FMAX - FMIN) // BLK
    size_list = FMIN + BLK * jax.random.randint(first_key, (FRONTS,), 0, steps_count + 1, dtype=jnp.int32)
    size_list = jnp.where(rank_order == 0, FMAX, size_list)
    size_list = jnp.where(rank_order == 1, FMIN, size_list)
    return size_list.astype(jnp.int32)


def shuffled_fronts(one_key):
    return jax.random.permutation(one_key, FRONTS)


def layout_targets(key):
    row_count = CYCLE // BLK
    first_key, rank_order = rank_of_fronts(key)
    front_ids = jnp.arange(FRONTS, dtype=jnp.int32)
    largest = jnp.sum(jnp.where(rank_order == 0, front_ids, 0)).astype(jnp.int32)
    route_key = jax.random.fold_in(key, 8)
    route_keys = jax.random.split(route_key, FRONTS * row_count)
    orders = jax.vmap(shuffled_fronts)(route_keys).astype(jnp.int32)
    first_order = orders[0]
    leading = first_order[0]
    fixed_order = jnp.where(front_ids == 0, largest, jnp.where(first_order == largest, leading, first_order))
    orders = orders.at[0].set(fixed_order)
    chosen = orders[:, :KB].reshape(FRONTS, row_count, KB)
    return jnp.transpose(chosen, (0, 2, 1)).astype(jnp.int32)


def draw_front_sizes(key, part):
    return layout_sizes(key)


def draw_dest_front(key, part):
    return layout_targets(key)


def draw_dest_local(key, part):
    row_count = CYCLE // BLK
    size_list = layout_sizes(key)
    targets = layout_targets(key)
    parent = size_list[targets]
    row_index = jnp.arange(row_count, dtype=jnp.int32)[None, None, :]
    lowest = jnp.maximum(0, (NPANEL * PW // BLK - row_index + row_count - 1) // row_count)
    highest = (parent // BLK - 1 - row_index) // row_count
    local_key = jax.random.fold_in(key, 9)
    lowest = jnp.broadcast_to(lowest, (FRONTS, KB, row_count))
    drawn = jax.random.randint(local_key, (FRONTS, KB, row_count), lowest, highest + 1, dtype=jnp.int32)
    first_slot = (jnp.arange(FRONTS)[:, None, None] == 0) & (jnp.arange(KB)[None, :, None] == 0) & (jnp.arange(row_count)[None, None, :] == 0)
    return jnp.where(first_slot, highest, drawn).astype(jnp.int32)


def draw_front_matrix(key, part):
    full_shape = (FRONTS, LOCB, CYCLE, W)
    normal_key, level_key = jax.random.split(key)
    entries = jax.random.normal(normal_key, full_shape, jnp.float32)
    global_row = jnp.arange(LOCB)[:, None] * CYCLE + jnp.arange(CYCLE)[None, :]
    on_diagonal = global_row[:, :, None] == jnp.arange(W)[None, None, :]
    diagonal_level = jax.random.uniform(level_key, full_shape, jnp.float32, 96.0, 192.0)
    return jnp.where(on_diagonal[None], diagonal_level, entries)


def block_scale(own_key, dims, shards, smallest, high):
    gain = 1.0
    for position, parts in shards:
        draws = jax.random.uniform(jax.random.fold_in(jax.random.fold_in(own_key, 6), position), (parts,), jnp.float32, smallest / len(shards), high / len(shards))
        gain = gain * jnp.repeat(jnp.exp(draws), dims[position] // parts).reshape((-1,) + (1,) * (len(dims) - 1 - position))
    return gain


def bell_draw(stream_key, shape, spread, reach, pieces=(), held_as=jnp.bfloat16):
    values = jax.random.normal(stream_key, shape, jnp.float32) * spread
    if len(pieces) > 0:
        values = block_scale(stream_key, shape, pieces, -0.22, 0.18) * values
    return jnp.clip(values, min=-reach, max=reach).astype(held_as)


def setup_inputs(seed: int = 0) -> dict:
    seeds = jax.random.split(jax.random.key(seed), 6)
    return {
        "front_matrix": draw_front_matrix(jax.random.fold_in(seeds[5], 71), 0),
        "front_sizes": draw_front_sizes(jax.random.fold_in(seeds[5], 71), 0),
        "contrib": bell_draw(seeds[2], (FRONTS, KB, CYCLE, W), 1.0, 6.0, ((0, 4), (2, 4), (3, 2)), jnp.float32),
        "dest_front": draw_dest_front(jax.random.fold_in(seeds[5], 71), 0),
        "dest_local": draw_dest_local(jax.random.fold_in(seeds[5], 71), 0),
    }


def lower_inverse(pivot_block):
    symmetric = jnp.tril(pivot_block) + jnp.tril(pivot_block, -1).T
    factor = jnp.linalg.cholesky(symmetric)
    eye_block = jnp.eye(factor.shape[0], dtype=factor.dtype)
    inverse = jax.scipy.linalg.solve_triangular(factor, eye_block, lower=True)
    return (factor, inverse)

def factor_front(front_rows):
    global_row = jnp.arange(FMAX, dtype=jnp.int32)
    for panel_index in range(NPANEL):
        col_start = panel_index * PW
        factor, inverse = lower_inverse(front_rows[col_start:col_start + PW, col_start:col_start + PW])
        solved = jnp.dot(front_rows[:, col_start:col_start + PW], inverse.T, precision=lax.Precision.HIGHEST)
        solved = jnp.where((global_row < col_start)[:, None], 0.0, solved)
        solved = solved.at[col_start:col_start + PW].set(factor)
        later_rows = solved[col_start + PW:W]
        update = jnp.dot(solved, later_rows.T, precision=lax.Precision.HIGHEST)
        trailing = front_rows[:, col_start + PW:] - jnp.where((global_row >= col_start + PW)[:, None], update, 0.0)
        front_rows = jnp.concatenate([front_rows[:, :col_start], solved, trailing], axis=1)
    front_rows = front_rows.at[:NPANEL * PW, NPANEL * PW:].set(0.0)
    return front_rows

def assemble(front_index, front_block, size_now, blocks, targets, places):
    row_count = CYCLE // BLK
    front_rows = front_block.reshape(FMAX, W)
    global_row = jnp.arange(FMAX, dtype=jnp.int32)
    front_rows = jnp.where((global_row < size_now)[:, None], front_rows, 0.0)

    def add_block(index, current):
        row_start = ((places[index] * row_count + index % row_count) * BLK).astype(jnp.int32)
        present = lax.dynamic_slice_in_dim(current, row_start, BLK, 0)
        arriving = jnp.where(targets[index] == front_index, blocks[index], 0.0)
        return lax.dynamic_update_slice_in_dim(current, present + arriving, row_start, 0)
    return lax.fori_loop(0, blocks.shape[0], add_block, front_rows)

def reference(front_matrix, front_sizes, contrib, dest_front, dest_local):
    row_count = CYCLE // BLK
    blocks = contrib.reshape(FRONTS * KB * row_count, BLK, W)
    targets = dest_front.reshape(-1)
    places = dest_local.reshape(-1)

    def one_front(front_index):
        assembled = assemble(front_index, front_matrix[front_index], front_sizes[front_index], blocks, targets, places)
        return factor_front(assembled).reshape(LOCB, CYCLE, W)
    return lax.map(one_front, jnp.arange(FRONTS, dtype=jnp.int32))
```

```python
import functools

import jax
import jax.numpy as jnp
from jax import lax
from jax.experimental import pallas as pl
from jax.experimental.pallas import tpu as pltpu
from jax.sharding import PartitionSpec as P

PW = 512
NPANEL = 2
B = 128
KP = PW * NPANEL
NB = PW // B
NT = ((1,), (1,))
NN = ((1,), (0,))
TN = ((0,), (0,))
F32 = jnp.float32
BF16 = jnp.bfloat16
VMEM_LIMIT = 56 * 2**20


def split(x):
    high = x.astype(BF16)
    return high, (x - high.astype(F32)).astype(BF16)


def dot3(a, b, dims):
    def one(u, v):
        return lax.dot_general(u, v, (dims, ((), ())), preferred_element_type=F32)

    return one(a[0], b[0]) + (one(a[0], b[1]) + one(a[1], b[0]))


def dot6(a, b, dims):
    return lax.dot_general(
        a, b, (dims, ((), ())), precision=lax.Precision.HIGHEST, preferred_element_type=F32
    )


def over_lanes(group, lane):
    return jnp.broadcast_to(group[:, lane : lane + 1], group.shape)


def over_rows(group, row):
    return jnp.broadcast_to(group[row : row + 1, :], group.shape)


def factor_block(s_ref, v_ref, u_ref):
    sub = lax.broadcasted_iota(jnp.int32, (8, B), 0)
    lane = lax.broadcasted_iota(jnp.int32, (8, B), 1)
    n = B // 8
    left = [s_ref[8 * g : 8 * g + 8, :] for g in range(n)]
    right = [jnp.where(lane == sub + 8 * g, 1.0, 0.0).astype(F32) for g in range(n)]
    for b in range(n):
        cols = [[over_lanes(left[g], 8 * b + j) for j in range(8)] for g in range(b, n)]
        scale = jnp.ones((8, B), F32)
        for j in range(8):
            pivot = over_rows(cols[0][j], j)
            inv = 1.0 / pivot
            lrow = over_rows(left[b], j)
            rrow = over_rows(right[b], j)
            krow = [over_rows(cols[0][k], j) if k > j else None for k in range(8)]
            scale = jnp.where(sub == j, lax.rsqrt(pivot), scale)
            for g in range(b, n):
                f = cols[g - b][j] * inv
                if g == b:
                    f = jnp.where(sub > j, f, 0.0)
                for k in range(j + 1, 8):
                    cols[g - b][k] = cols[g - b][k] - f * krow[k]
                left[g] = left[g] - f * lrow
                right[g] = right[g] - f * rrow
        u_ref[8 * b : 8 * b + 8, :] = jnp.where(lane >= sub + 8 * b, left[b] * scale, 0.0)
        v_ref[8 * b : 8 * b + 8, :] = right[b] * scale


def panel_factor(m_ref, u_ref, v_ref):
    def body(k, _):
        c = pl.multiple_of(k * B, B)
        factor_block(m_ref.at[pl.ds(c, B), pl.ds(c, B)], v_ref, u_ref)
        row = dot6(v_ref[...], m_ref[pl.ds(c, B), :], NN)
        m_ref[pl.ds(c, B), :] = row
        m_ref[pl.ds(c, B), pl.ds(c, B)] = u_ref[...]
        for i in range(1, NB):

            @pl.when(i > k)
            def _():
                up = m_ref[pl.ds(c, B), i * B : (i + 1) * B]
                rows = slice(i * B, (i + 1) * B)
                m_ref[rows, :] = m_ref[rows, :] - dot6(up, row, TN)

        return 0

    lax.fori_loop(0, NB, body, 0)


def load_symmetric(a_ref, m_ref, col):
    r = lax.broadcasted_iota(jnp.int32, (B, B), 0)
    c = lax.broadcasted_iota(jnp.int32, (B, B), 1)
    for i in range(NB):
        for j in range(NB):
            here = (slice(i * B, (i + 1) * B), slice(PW + j * B, PW + (j + 1) * B))
            m_ref[here] = jnp.where(r == c, 1.0, 0.0) if i == j else jnp.zeros((B, B), F32)
            if j > i:
                continue
            block = a_ref[i * B : (i + 1) * B, col + j * B : col + (j + 1) * B]
            if i == j:
                block = jnp.where(r >= c, block, block.T)
                m_ref[i * B : (i + 1) * B, i * B : (i + 1) * B] = block
            else:
                m_ref[i * B : (i + 1) * B, j * B : (j + 1) * B] = block
                m_ref[j * B : (j + 1) * B, i * B : (i + 1) * B] = block.T


def store_factor(m_ref, l_ref, i_ref):
    for i in range(NB):
        for j in range(NB):
            here = (slice(i * B, (i + 1) * B), slice(j * B, (j + 1) * B))
            if j <= i:
                l_ref[here] = m_ref[j * B : (j + 1) * B, i * B : (i + 1) * B].T
            else:
                l_ref[here] = jnp.zeros((B, B), F32)
    i_ref[...] = m_ref[:, PW:]


def put_rows(me, refs, dst, first, count, cols, pick=None):
    exact = len(refs) == count
    for k, ref in enumerate(refs):
        at = (me ^ k) - first

        def store(ref=ref, at=at):
            value = ref[:, cols] if pick is None else ref[pick, :, cols]
            dst[pl.ds(pl.multiple_of(at * B, B), B), :] = value

        if exact:
            store()
        else:
            pl.when((at >= 0) & (at < count))(store)


def chol0_kernel(rows, info, *refs):
    pieces, (l_ref, i_ref, a_ref, m_ref, u_ref, v_ref) = refs[:rows], refs[rows:]

    @pl.when(info[0] == 0)
    def _():
        put_rows(info[1], pieces, a_ref, 0, NB, slice(0, PW))
        load_symmetric(a_ref, m_ref, 0)
        panel_factor(m_ref, u_ref, v_ref)
        store_factor(m_ref, l_ref, i_ref)


def middle_kernel(rows, first, info, i0_ref, *refs):
    pieces, (f_ref, a_ref) = refs[:rows], refs[rows:]

    @pl.when(info[0] == 0)
    def _():
        put_rows(info[1], pieces, a_ref, first, NB, slice(0, PW))
        f_ref[0] = i0_ref[...]
        f_ref[1] = dot6(a_ref[...], i0_ref[...], NT)


def chol1_kernel(rows, first, info, f_ref, *refs):
    pieces, (l_ref, i_ref, a_ref, m_ref, u_ref, v_ref) = refs[:rows], refs[rows:]

    @pl.when(info[0] == 0)
    def _():
        put_rows(info[1], pieces, a_ref, first, NB, slice(PW, KP))
        load_symmetric(a_ref, m_ref, 0)
        m_ref[:, :PW] = m_ref[:, :PW] - dot6(f_ref[1], f_ref[1], NT)
        panel_factor(m_ref, u_ref, v_ref)
        store_factor(m_ref, l_ref, i_ref)


def add_blocks(info, blocks, lb, store):
    for d, block in enumerate(blocks):

        @pl.when(info[4 + d] == lb)
        def _():
            store(block)


def window_kernel(fronts, span_a, span_b, info, p_ref, *refs):
    blocks, (a0, b0, a1, b1, t_ref) = refs[:fronts], refs[fronts:]

    @pl.when(info[0] == 1)
    def _():
        for lb in range(span_a[0], span_b[1]):
            t_ref[...] = p_ref[lb]

            def add(block):
                t_ref[...] += block[...]

            add_blocks(info, blocks, lb, add)
            for span, first, second in ((span_a, a0, a1), (span_b, b0, b1)):
                if span[0] <= lb < span[1]:
                    first[lb - span[0]] = t_ref[:, :PW]
                    second[lb - span[0]] = t_ref[:, PW:]


def fill_panel(info, blocks, i, g, rows, p_ref, t_ref):
    for l in range(g):
        lb = i * g + l
        span = slice(l * B, (l + 1) * B)
        valid = (lb * rows + info[1]) * B < info[2]
        t_ref[span, :] = jnp.where(valid, p_ref[l, :, :KP], 0.0)

        def add(block):
            t_ref[span, :] += block[...]

        add_blocks(info, blocks, lb, add)


def update0_kernel(sizes, info, *refs):
    rows, fronts, g, nb, first = sizes
    f_ref, refs = refs[0], refs[1:]
    w0, w1, blocks = refs[:rows], refs[rows : 2 * rows], refs[2 * rows : 2 * rows + fronts]
    p_ref, x_ref, t_out, p_high, p_low, w_out = refs[2 * rows + fronts : 2 * rows + fronts + 6]
    w_s, t_s, i_high, i_low, z_high, z_low, y_high, y_low = refs[2 * rows + fronts + 6 :]
    i = pl.program_id(0)
    half = y_high.shape[0]

    @pl.when(info[0] == 1)
    def _():
        @pl.when(i == 0)
        def _():
            for pieces, dst in ((w0, w_s), (w1, w_out)):
                for l in range(nb):
                    put_rows(info[1], pieces, dst, first - l * rows, half // B, slice(0, PW), l) if (
                        first
                    ) else put_at(info[1], pieces, dst, l * rows, l)
            i_high[...], i_low[...] = split(f_ref[0])
            inverse = (i_high[...], i_low[...])
            z_high[...], z_low[...] = split(dot3(split(f_ref[1]), inverse, NN))
            z = (z_high[...], z_low[...])
            for n in range(half // PW):
                span = slice(n * PW, (n + 1) * PW)
                w = split(w_s[span, :])
                x = split(dot3(w, inverse, NT))
                y_high[span, :], y_low[span, :] = split(dot3(x, inverse, NN))
                w_out[span, :] = w_out[span, :] - dot3(w, z, NT)

        fill_panel(info, blocks, i, g, rows, p_ref, t_s)
        p = split(t_s[:, :PW])
        later = t_s[:, PW:] - dot3(p, (z_high[...], z_low[...]), NT)
        high, low = split(later)
        p_high[...] = high.reshape(p_high.shape)
        p_low[...] = low.reshape(p_low.shape)
        for n in range(half // PW):
            span = slice(n * PW, (n + 1) * PW)
            update = dot3(p, (y_high[span, :], y_low[span, :]), NT)
            for l in range(g):
                valid = ((i * g + l) * rows + info[1]) * B < info[2]
                t_out[l, :, span] = (
                    jnp.where(valid, x_ref[l, :, span], 0.0) - update[l * B : (l + 1) * B]
                )


def put_at(me, refs, dst, base, pick):
    for k, ref in enumerate(refs):
        at = (me ^ k) + base
        dst[pl.ds(pl.multiple_of(at * B, B), B), :] = ref[pick]


def final_kernel(sizes, info, *refs):
    rows, fronts, g, npl, na, first_a = sizes
    f_ref, i1_ref, l0_ref, l1_ref, i1r_ref, wn_ref = refs[:6]
    refs = refs[6:]
    w0, w1, blocks = refs[:rows], refs[rows : 2 * rows], refs[2 * rows : 2 * rows + fronts]
    x_ref, t_ref, p_high, p_low, out = refs[2 * rows + fronts : 2 * rows + fronts + 5]
    refs = refs[2 * rows + fronts + 5 :]
    t_s, w0_s, w1_s, i0, l10, i1, x0w, x1w, y_high, y_low = refs
    i = pl.program_id(0)
    half = y_high.shape[0]

    @pl.when(info[0] == 0)
    def _():
        @pl.when(i == 0)
        def _():
            for pieces, dst in ((w0, w0_s), (w1, w1_s)):
                put_rows(info[1], pieces, dst, first_a, NB, slice(0, PW), 0)
            for value, dst in ((f_ref[0], i0), (f_ref[1], l10), (i1_ref[...], i1)):
                dst[0], dst[1] = split(value)
            x = split(dot3(split(w0_s[...]), (i0[0], i0[1]), NT))
            x0w[0], x0w[1] = x
            later = split(w1_s[...] - dot3(x, (l10[0], l10[1]), NT))
            x1w[0], x1w[1] = split(dot3(later, (i1[0], i1[1]), NT))

        fill_panel(info, blocks, i, g, rows, x_ref, t_s)
        x0 = dot3(split(t_s[:, :PW]), (i0[0], i0[1]), NT)
        x0s = split(x0)
        later = split(t_s[:, PW:] - dot3(x0s, (l10[0], l10[1]), NT))
        x1 = dot3(later, (i1[0], i1[1]), NT)
        update = dot3(x0s, (x0w[0], x0w[1]), NT) + dot3(split(x1), (x1w[0], x1w[1]), NT)
        for l in range(g):
            span = slice(l * B, (l + 1) * B)
            valid = ((i * g + l) * rows + info[1]) * B < info[2]
            out[l, :, :PW] = x0[span]
            out[l, :, PW:KP] = x1[span]
            out[l, :, KP:] = jnp.where(valid, x_ref[l, :, KP:], 0.0) - update[span]

        @pl.when(i == 0)
        def _():
            for l in range(npl):
                row = (l * rows + info[1]) * B
                out[l, :, KP:] = jnp.zeros((B, half - KP), F32)

                @pl.when(row < PW)
                def _():
                    out[l, :, :PW] = l0_ref[pl.ds(pl.multiple_of(row, B), B), :]
                    out[l, :, PW:KP] = jnp.zeros((B, PW), F32)

                @pl.when(row >= PW)
                def _():
                    at = pl.ds(pl.multiple_of(row - PW, B), B)
                    out[l, :, :PW] = f_ref[1, at, :]
                    out[l, :, PW:KP] = l1_ref[at, :]

    @pl.when(info[0] == 1)
    def _():
        @pl.when(i == 0)
        def _():
            i1[0], i1[1] = split(i1r_ref[...])
            inverse = (i1[0], i1[1])
            for n in range(half // PW):
                span = slice(n * PW, (n + 1) * PW)
                x = split(dot3(split(wn_ref[span, :]), inverse, NT))
                y_high[span, :], y_low[span, :] = split(dot3(x, inverse, NN))

        p = (p_high[...].reshape(g * B, PW), p_low[...].reshape(g * B, PW))
        for n in range(half // PW):
            span = slice(n * PW, (n + 1) * PW)
            update = dot3(p, (y_high[span, :], y_low[span, :]), NT)
            for l in range(g):
                out[l, :, span] = t_ref[l, :, span] - update[l * B : (l + 1) * B]

        @pl.when(i == 0)
        def _():
            for l in range(npl):
                out[l] = jnp.zeros((B, half), F32)


def add_kernel(fronts, info, _, *refs):
    wide, narrow = refs[:fronts], refs[fronts : 2 * fronts]
    out, buf, sem_in, sem_out = refs[2 * fronts :]

    def firsts():
        for s in range(fronts):
            place = info[4 + s]
            first = place >= 0
            for e in range(s):
                first = first & (info[4 + e] != place)
            yield s, place, first

    for s, place, first in firsts():

        @pl.when(first)
        def _():
            pltpu.make_async_copy(out.at[place], buf.at[s], sem_in.at[s]).start()

    for s, place, first in firsts():

        @pl.when(first)
        def _():
            pltpu.make_async_copy(out.at[place], buf.at[s], sem_in.at[s]).wait()
            for e in range(s, fronts):

                @pl.when(info[4 + e] == place)
                def _():
                    buf[s, :, KP:] += narrow[e][...]

                    @pl.when(info[0] == 1)
                    def _():
                        buf[s, :, :KP] += wide[e][...]

            pltpu.make_async_copy(buf.at[s], out.at[place], sem_out.at[s]).start()

    for s, place, first in firsts():

        @pl.when(first)
        def _():
            pltpu.make_async_copy(buf.at[s], out.at[place], sem_out.at[s]).wait()


WHOLE = pl.BlockSpec(memory_space=pltpu.VMEM)
SCALARS = pl.BlockSpec(memory_space=pltpu.SMEM)
PARAMS = pltpu.CompilerParams(vmem_limit_bytes=VMEM_LIMIT)


def shape(*dims, dtype=F32):
    return jax.ShapeDtypeStruct(dims, dtype)


def after(value, *others):
    return lax.optimization_barrier((value, *others))[0]


def on_device(front_matrix, front_sizes, contrib, dest_front, dest_local):
    fronts = lax.axis_size("front")
    rows = lax.axis_size("row")
    front_here = lax.axis_index("front")
    row_here = lax.axis_index("row")
    col_here = lax.axis_index("col")
    matrix = front_matrix[0]
    blocks_here, _, half = matrix.shape
    npl = KP // (rows * B)
    g = max(1, blocks_here // 6)
    tiles = blocks_here // g
    span_a = (KP // B // rows, (half // B - 1) // rows + 1)
    span_b = (half // B // rows, (2 * half // B - 1) // rows + 1)
    first_a = KP // B - span_a[0] * rows
    first_b = half // B - span_b[0] * rows
    na, nb = span_a[1] - span_a[0], span_b[1] - span_b[0]

    def rows_from(x, source, target):
        moved = []
        for k in range(rows):
            if k == 0 and source == target:
                moved.append(x)
                continue
            pairs = [(r * 2 + source, (r ^ k) * 2 + target) for r in range(rows)]
            moved.append(lax.ppermute(x, ("row", "col"), pairs))
        return moved

    def along_fronts(x, d, source, target):
        pairs = [(f * 2 + s, (f + d) % fronts * 2 + t) for f in range(fronts) for s, t in zip(source, target)]
        return lax.ppermute(x, ("front", "col"), pairs)

    def to_other(x, source):
        return lax.ppermute(x, "col", [(source, 1 - source)])

    if npl == 2:
        pivot0 = rows_from(matrix[0, :, :PW], 0, 0)
        pivot1 = rows_from(matrix[1, :, :KP], 0, 0)
        first1 = 0
    else:
        pivot0 = pivot1 = rows_from(matrix[0, :, :KP], 0, 0)
        first1 = NB

    targets = dest_front[0, :, 0]
    places = dest_local[0, :, 0]
    fronts_all = jnp.arange(fronts, dtype=jnp.int32)
    select = targets[None, :] == fronts_all[:, None]
    slot = jnp.argmax(select, axis=1).astype(jnp.int32)
    slot_place = jnp.where(
        jnp.any(select, axis=1), jnp.sum(jnp.where(select, places[None, :], 0), axis=1), -1
    ).astype(jnp.int32)
    in_place = lax.all_to_all(slot_place, "front", split_axis=0, concat_axis=0, tiled=True)
    order = (front_here - fronts_all) % fronts
    info = jnp.concatenate(
        [
            jnp.stack([col_here, row_here, front_sizes[0], 0]).astype(jnp.int32),
            in_place[order],
        ]
    )
    slots = slot[(front_here + fronts_all) % fronts]

    def block(d, start, width):
        return lax.dynamic_slice(contrib[0], (slots[d], 0, start), (1, B, width))[0]

    panel_raw = to_other(matrix[:, :, :KP], 0)
    panel_blocks = [along_fronts(block(d, 0, KP), d, (0,), (1,)) for d in range(fronts)]

    l0, i0 = pl.pallas_call(
        functools.partial(chol0_kernel, rows),
        out_shape=[shape(PW, PW)] * 2,
        in_specs=[SCALARS] + [WHOLE] * rows,
        out_specs=[WHOLE] * 2,
        scratch_shapes=[
            pltpu.VMEM((PW, PW), F32),
            pltpu.VMEM((PW, 2 * PW), F32),
            pltpu.VMEM((B, B), F32),
            pltpu.VMEM((B, B), F32),
        ],
        compiler_params=PARAMS,
        name="factor0",
    )(info, *pivot0)
    fi = pl.pallas_call(
        functools.partial(middle_kernel, rows, first1),
        out_shape=shape(2, PW, PW),
        in_specs=[SCALARS] + [WHOLE] * (rows + 1),
        out_specs=WHOLE,
        scratch_shapes=[pltpu.VMEM((PW, PW), F32)],
        compiler_params=PARAMS,
        name="middle",
    )(info, i0, *pivot1)

    window = pl.pallas_call(
        functools.partial(window_kernel, fronts, span_a, span_b),
        out_shape=[shape(na, B, PW), shape(nb, B, PW)] * 2,
        grid=(1,),
        in_specs=[SCALARS, pl.BlockSpec((span_b[1], B, KP), lambda i: (0, 0, 0))] + [WHOLE] * fronts,
        out_specs=[WHOLE] * 4,
        scratch_shapes=[pltpu.VMEM((B, KP), F32)],
        compiler_params=PARAMS,
        name="window",
    )(info, after(panel_raw, fi), *panel_blocks)
    wa0, wb0, wa1, wb1 = window
    wb0 = rows_from(wb0, 1, 1)
    wa0 = rows_from(wa0, 1, 0)
    wb1 = rows_from(wb1, 1, 1)
    wa1 = rows_from(wa1, 1, 0)
    fi_other = to_other(after(fi, *window), 0)
    panel_back = [to_other(after(x, *window), 1) for x in panel_blocks]
    wide = [after(block(0, 0, KP), *window)]
    narrow = [after(block(0, KP, half - KP), *window)]
    for d in range(1, fronts):
        wide.append(along_fronts(after(block(d, 0, KP), *window), d, (1,), (1,)))
        narrow.append(along_fronts(after(block(d, KP, half - KP), *window), d, (0, 1), (0, 1)))

    l1, i1 = pl.pallas_call(
        functools.partial(chol1_kernel, rows, first1),
        out_shape=[shape(PW, PW)] * 2,
        in_specs=[SCALARS] + [WHOLE] * (rows + 1),
        out_specs=[WHOLE] * 2,
        scratch_shapes=[
            pltpu.VMEM((PW, PW), F32),
            pltpu.VMEM((PW, 2 * PW), F32),
            pltpu.VMEM((B, B), F32),
            pltpu.VMEM((B, B), F32),
        ],
        compiler_params=PARAMS,
        name="factor1",
    )(info, after(fi, *window), *pivot1)

    def tile(width, core):
        return pl.BlockSpec((g, B, width), lambda i, s: (jnp.where(s[0] == core, i, 0), 0, 0))

    trailing, p_high, p_low, w_next = pl.pallas_call(
        functools.partial(update0_kernel, (rows, fronts, g, nb, first_b)),
        out_shape=[
            shape(blocks_here, B, half),
            shape(blocks_here, B, PW, dtype=BF16),
            shape(blocks_here, B, PW, dtype=BF16),
            shape(half, PW),
        ],
        grid_spec=pltpu.PrefetchScalarGridSpec(
            num_scalar_prefetch=1,
            grid=(tiles,),
            in_specs=[WHOLE] * (1 + 2 * rows + fronts) + [tile(KP, 1), tile(half, 1)],
            out_specs=[tile(half, 1), tile(PW, 1), tile(PW, 1), WHOLE],
            scratch_shapes=[
                pltpu.VMEM((half, PW), F32),
                pltpu.VMEM((g * B, KP), F32),
                pltpu.VMEM((PW, PW), BF16),
                pltpu.VMEM((PW, PW), BF16),
                pltpu.VMEM((PW, PW), BF16),
                pltpu.VMEM((PW, PW), BF16),
                pltpu.VMEM((half, PW), BF16),
                pltpu.VMEM((half, PW), BF16),
            ],
        ),
        compiler_params=PARAMS,
        name="update0",
    )(info, after(fi_other, i1), *wb0, *wb1, *panel_blocks, panel_raw, matrix)
    i1_other = to_other(i1, 0)

    pair = pltpu.VMEM((2, PW, PW), BF16)
    out = pl.pallas_call(
        functools.partial(final_kernel, (rows, fronts, g, npl, na, first_a)),
        out_shape=shape(blocks_here, B, half),
        grid_spec=pltpu.PrefetchScalarGridSpec(
            num_scalar_prefetch=1,
            grid=(tiles,),
            in_specs=[WHOLE] * (6 + 2 * rows + fronts) + [tile(half, 0), tile(half, 1), tile(PW, 1), tile(PW, 1)],
            out_specs=pl.BlockSpec((g, B, half), lambda i, s: (i, 0, 0)),
            scratch_shapes=[
                pltpu.VMEM((g * B, KP), F32),
                pltpu.VMEM((PW, PW), F32),
                pltpu.VMEM((PW, PW), F32),
                pair,
                pair,
                pair,
                pair,
                pair,
                pltpu.VMEM((half, PW), BF16),
                pltpu.VMEM((half, PW), BF16),
            ],
        ),
        compiler_params=PARAMS,
        name="final",
    )(info, fi, i1, l0, l1, i1_other, w_next, *wa0, *wa1, *panel_back, matrix, trailing, p_high, p_low)

    out = pl.pallas_call(
        functools.partial(add_kernel, fronts),
        out_shape=shape(blocks_here, B, half),
        in_specs=[SCALARS, pl.BlockSpec(memory_space=pl.ANY)] + [WHOLE] * (2 * fronts),
        out_specs=pl.BlockSpec(memory_space=pl.ANY),
        scratch_shapes=[
            pltpu.VMEM((fronts, B, half), F32),
            pltpu.SemaphoreType.DMA((fronts,)),
            pltpu.SemaphoreType.DMA((fronts,)),
        ],
        input_output_aliases={1: 0},
        compiler_params=PARAMS,
        name="add",
    )(info, out, *wide, *narrow)
    return out[None]


def solution(mesh):
    return jax.shard_map(
        on_device,
        mesh=mesh,
        in_specs=(
            P("front", None, "row", "col"),
            P("front"),
            P("front", None, "row", "col"),
            P("front", None, "row"),
            P("front", None, "row"),
        ),
        out_specs=P("front", None, "row", "col"),
        check_vma=False,
    )
```

```python
import functools

import jax
import jax.numpy as jnp
from jax import lax
from jax.experimental import pallas as pl
from jax.experimental.pallas import tpu as pltpu
from jax.sharding import PartitionSpec as P

PW = 512
NPANEL = 2
B = 128
KP = PW * NPANEL
NB = PW // B
EXT = B + 8
NT = ((1,), (1,))
NN = ((1,), (0,))
TN = ((0,), (0,))
F32 = jnp.float32
BF16 = jnp.bfloat16
VMEM_LIMIT = 56 * 2**20


def split(x):
    high = x.astype(BF16)
    return high, (x - high.astype(F32)).astype(BF16)


def dot3(a, b, dims):
    def one(u, v):
        return lax.dot_general(u, v, (dims, ((), ())), preferred_element_type=F32)

    return one(a[0], b[0]) + (one(a[0], b[1]) + one(a[1], b[0]))


def dot6(a, b, dims):
    return lax.dot_general(
        a, b, (dims, ((), ())), precision=lax.Precision.HIGHEST, preferred_element_type=F32
    )


def over_lanes(group, lane):
    return jnp.broadcast_to(group[:, lane : lane + 1], group.shape)


def over_rows(group, row):
    return jnp.broadcast_to(group[row : row + 1, :], group.shape)


def factor_block(s_ref, v_ref, u_ref):
    sub = lax.broadcasted_iota(jnp.int32, (8, B), 0)
    lane = lax.broadcasted_iota(jnp.int32, (8, B), 1)
    n = B // 8
    left = [s_ref[8 * g : 8 * g + 8, :] for g in range(n)]
    right = [jnp.where(lane == sub + 8 * g, 1.0, 0.0).astype(F32) for g in range(n)]
    for b in range(n):
        cols = [[over_lanes(left[g], 8 * b + j) for j in range(8)] for g in range(b, n)]
        scale = jnp.ones((8, B), F32)
        for j in range(8):
            pivot = over_rows(cols[0][j], j)
            inv = 1.0 / pivot
            lrow = over_rows(left[b], j)
            rrow = over_rows(right[b], j)
            krow = [over_rows(cols[0][k], j) if k > j else None for k in range(8)]
            scale = jnp.where(sub == j, lax.rsqrt(pivot), scale)
            for g in range(b, n):
                f = cols[g - b][j] * inv
                if g == b:
                    f = jnp.where(sub > j, f, 0.0)
                for k in range(j + 1, 8):
                    cols[g - b][k] = cols[g - b][k] - f * krow[k]
                left[g] = left[g] - f * lrow
                right[g] = right[g] - f * rrow
        u_ref[8 * b : 8 * b + 8, :] = jnp.where(lane >= sub + 8 * b, left[b] * scale, 0.0)
        v_ref[8 * b : 8 * b + 8, :] = right[b] * scale


def panel_factor(m_ref, u_ref, v_ref):
    def body(k, _):
        c = pl.multiple_of(k * B, B)
        factor_block(m_ref.at[pl.ds(c, B), pl.ds(c, B)], v_ref, u_ref)
        row = dot6(v_ref[...], m_ref[pl.ds(c, B), :], NN)
        m_ref[pl.ds(c, B), :] = row
        m_ref[pl.ds(c, B), pl.ds(c, B)] = u_ref[...]
        for i in range(1, NB):

            @pl.when(i > k)
            def _():
                up = m_ref[pl.ds(c, B), i * B : (i + 1) * B]
                rows = slice(i * B, (i + 1) * B)
                m_ref[rows, :] = m_ref[rows, :] - dot6(up, row, TN)

        return 0

    lax.fori_loop(0, NB, body, 0)


def load_symmetric(a_ref, m_ref, col):
    r = lax.broadcasted_iota(jnp.int32, (B, B), 0)
    c = lax.broadcasted_iota(jnp.int32, (B, B), 1)
    for i in range(NB):
        for j in range(NB):
            here = (slice(i * B, (i + 1) * B), slice(PW + j * B, PW + (j + 1) * B))
            m_ref[here] = jnp.where(r == c, 1.0, 0.0) if i == j else jnp.zeros((B, B), F32)
            if j > i:
                continue
            block = a_ref[i * B : (i + 1) * B, col + j * B : col + (j + 1) * B]
            if i == j:
                block = jnp.where(r >= c, block, block.T)
                m_ref[i * B : (i + 1) * B, i * B : (i + 1) * B] = block
            else:
                m_ref[i * B : (i + 1) * B, j * B : (j + 1) * B] = block
                m_ref[j * B : (j + 1) * B, i * B : (i + 1) * B] = block.T


def store_factor(m_ref, l_ref, i_ref):
    for i in range(NB):
        for j in range(NB):
            here = (slice(i * B, (i + 1) * B), slice(j * B, (j + 1) * B))
            if j <= i:
                l_ref[here] = m_ref[j * B : (j + 1) * B, i * B : (i + 1) * B].T
            else:
                l_ref[here] = jnp.zeros((B, B), F32)
    i_ref[...] = m_ref[:, PW:]


class Copies:
    def __init__(self, sems):
        self.sems, self.count = sems, 0

    def start(self, src, dst, when=None):
        copy = pltpu.make_async_copy(src, dst, self.sems.at[self.count])
        self.count += 1
        if when is None:
            copy.start()
        else:
            pl.when(when)(copy.start)
        return copy, when

    @staticmethod
    def wait(started):
        for copy, when in started:
            if when is None:
                copy.wait()
            else:
                pl.when(when)(copy.wait)


def take_rows(copies, me, pieces, dst, first, count, pick, cols):
    started = []
    rows = len(pieces)
    for k, piece in enumerate(pieces):
        for l, src in pick(piece):
            at = (me ^ k) + l * rows - first
            low, high = l * rows - first, l * rows - first + rows - 1
            inside = None if low >= 0 and high < count else (at >= 0) & (at < count)
            clipped = at if inside is None else jnp.clip(at, 0, count - 1)
            here = pl.ds(pl.multiple_of(clipped * B, B), B)
            started.append(copies.start(src, dst.at[here, cols], inside))
    return started


class Sizes:
    def __init__(self, rows, fronts, per_device, blocks_here, half):
        self.rows, self.fronts, self.kb = rows, fronts, per_device
        self.blocks, self.half = blocks_here, half
        self.npl = KP // (rows * B)
        self.g = max(1, blocks_here // 6)
        self.tiles = blocks_here // self.g
        self.windows = 2 * half // (rows * B) - self.npl
        self.pivot_first = 0 if self.npl == 2 else NB
        self.n0 = rows + 1 if rows == 4 and self.windows % 2 == 0 else rows
        self.a_first = KP // B
        self.a_count = (half - KP) // B
        self.b_first = half // B
        self.b_count = half // B

    def narrow_at(self, d):
        width = self.half - KP
        per = KP // width
        return (pl.ds(self.half - KP + d // per * B, B), pl.ds(d % per * width, width))

    def window_blocks(self, first, count):
        return range(first // self.rows - self.npl, (first + count - 1) // self.rows + 1 - self.npl)


def gathered(z, refs):
    if len(refs) == z.rows:
        return [lambda l, ref=ref: ref.at[l] for ref in refs]
    half = z.windows // 2
    whole, (first, second) = refs[: z.rows - 1], refs[z.rows - 1 :]
    across = lambda l: first.at[l] if l < half else second.at[l - half]
    return [lambda l, ref=ref: ref.at[l] for ref in whole] + [across]


def route(z, info, dest, d):
    front = lax.rem(info[3] + d, z.fronts)
    slot, place = jnp.int32(0), jnp.int32(-1)
    for k in range(z.kb):
        hit = dest[k] == front
        slot = jnp.where(hit, k, slot)
        place = jnp.where(hit, dest[z.kb + k], place)
    return slot, place


def read_places(z, blocks, places):
    for d in range(z.fronts):
        places[d] = jnp.max(blocks[d, B:EXT, :B]).astype(jnp.int32)


def factor0_kernel(z, info, *refs):
    pieces, (l_out, i_out, a_ref, m_ref, u_ref, v_ref, sems) = refs[: z.rows], refs[z.rows :]

    @pl.when(info[0] == 0)
    def _():
        copies = Copies(sems)
        pick = lambda piece: [(0, piece.at[:, pl.ds(0, PW)])]
        copies.wait(take_rows(copies, info[1], pieces, a_ref, 0, NB, pick, slice(None)))
        load_symmetric(a_ref, m_ref, 0)
        panel_factor(m_ref, u_ref, v_ref)
        store_factor(m_ref, l_out, i_out)


def middle_kernel(z, info, i0_ref, *refs):
    pieces, (out, a_ref, f_s, sems) = refs[: z.rows], refs[z.rows :]

    @pl.when(info[0] == 0)
    def _():
        copies = Copies(sems)
        pick = lambda piece: [(0, piece.at[:, pl.ds(0, PW)])]
        started = take_rows(copies, info[1], pieces, a_ref, z.pivot_first, NB, pick, slice(None))
        started.append(copies.start(i0_ref, f_s.at[:, pl.ds(0, PW)]))
        copies.wait(started)
        f_s[:, PW:] = dot6(a_ref[...], f_s[:, :PW], NT)
        copies.wait(
            [copies.start(f_s.at[pl.ds(n * B, B)], out.at[n, pl.ds(0, B)]) for n in range(NB)]
        )


def take_factor(copies, packed, f_s):
    return [copies.start(packed.at[n, pl.ds(0, B)], f_s.at[pl.ds(n * B, B)]) for n in range(NB)]


def sort_kernel(z, info, dest, first, second, *refs):
    f = z.fronts
    panel, late = refs[:f], refs[f : 2 * f]
    c_s, e_s, sems = refs[2 * f :]
    narrow = z.half - KP

    @pl.when(info[0] == 1)
    def _():
        copies = Copies(sems)
        routes = [route(z, info, dest, d) for d in range(f)]
        order = list(range(1, f)) + [0]
        reads = {}
        for d in order:
            slot, place = routes[d]
            c_s[d, B:EXT, :B] = jnp.full((EXT - B, B), place.astype(F32))
            reads[d] = copies.start(first.at[slot, :, pl.ds(0, KP)], c_s.at[d, pl.ds(0, B)])
        more = []
        for d in order:
            slot = routes[d][0]
            more.append(
                copies.start(first.at[slot, :, pl.ds(KP, narrow)], e_s.at[d, :, pl.ds(0, narrow)])
            )
            more.append(copies.start(second.at[slot], e_s.at[d, :, pl.ds(narrow, z.half)]))
        writes = []
        for d in order:
            copies.wait([reads[d]])
            writes.append(copies.start(c_s.at[d], panel[d]))
        for n, d in enumerate(order):
            copies.wait(more[2 * n : 2 * n + 2])
            writes.append(copies.start(e_s.at[d], late[d]))
        copies.wait(writes)


def window_kernel(z, info, other, _, *refs):
    f = z.fronts
    panel, (h0, h1, back), (t_ref, c_ref, places, sems) = refs[:f], refs[f : f + 3], refs[f + 3 :]

    @pl.when(info[0] == 1)
    def _():
        copies = Copies(sems)
        started = [copies.start(other.at[pl.ds(z.npl, z.windows), :, pl.ds(0, KP)], t_ref)]
        started += [copies.start(panel[d], c_ref.at[d]) for d in range(f)]
        copies.wait(started)
        later = [copies.start(c_ref, back)]
        read_places(z, c_ref, places)
        for d in range(f):
            place = places[d] - z.npl

            @pl.when((place >= 0) & (place < z.windows))
            def _():
                t_ref[place] += c_ref[d, :B]

        later.append(copies.start(t_ref.at[:, :, pl.ds(0, PW)], h0))
        later.append(copies.start(t_ref.at[:, :, pl.ds(PW, PW)], h1))
        copies.wait(later)


def fill_panel(z, info, places, blocks, i, p_ref, t_ref):
    for l in range(z.g):
        lb = i * z.g + l
        valid = (lb * z.rows + info[1]) * B < info[2]
        t_ref[l * B : (l + 1) * B, :] = jnp.where(valid, p_ref[l, :, :KP], 0.0)
    for d in range(z.fronts):
        at = places[d] - i * z.g

        @pl.when((at >= 0) & (at < z.g))
        def _():
            here = pl.ds(pl.multiple_of(at * B, B), B)
            t_ref[here, :] += blocks[d, :B]


def both_kernel(z, info, mine, theirs, *refs):
    pivots, w0, refs = refs[: z.rows], refs[z.rows : z.rows + z.n0], refs[z.rows + z.n0 :]
    p_ref, x_ref, l_out, i_out, t_out, p_high, p_low, z_out = refs[:8]
    a_ref, f_s, i_s, m_ref, u_ref, v_ref, w_s, t_s, c_s, inv, y, places, sems = refs[8:]
    i = pl.program_id(0)

    @pl.when((info[0] == 0) & (i == 0))
    def _():
        copies = Copies(sems)
        pick = lambda piece: [(0, piece.at[:, pl.ds(PW, PW)])]
        started = take_rows(copies, info[1], pivots, a_ref, z.pivot_first, NB, pick, slice(None))
        started += take_factor(copies, mine, f_s)
        copies.wait(started)
        load_symmetric(a_ref, m_ref, 0)
        m_ref[:, :PW] = m_ref[:, :PW] - dot6(f_s[:, PW:], f_s[:, PW:], NT)
        panel_factor(m_ref, u_ref, v_ref)
        store_factor(m_ref, l_out, i_s)
        copies.wait([copies.start(i_s, i_out.at[pl.ds(0, PW), pl.ds(0, PW)])])

    @pl.when(info[0] == 1)
    def _():
        @pl.when(i == 0)
        def _():
            copies = Copies(sems)
            used = z.window_blocks(z.b_first, z.b_count)
            pick = lambda piece: [(l + z.npl, piece(l)) for l in used]
            started = take_rows(copies, info[1], gathered(z, w0), w_s, z.b_first, z.b_count, pick, slice(None))
            started += take_factor(copies, theirs, f_s)
            started.append(copies.start(mine, c_s))
            copies.wait(started)
            read_places(z, c_s, places)
            inv[0], inv[1] = split(f_s[:, :PW])
            inverse = (inv[0], inv[1])
            z_out[0], z_out[1] = split(dot3(split(f_s[:, PW:]), inverse, NN))
            for n in range(z.half // PW):
                span = slice(n * PW, (n + 1) * PW)
                x = split(dot3(split(w_s[span, :]), inverse, NT))
                y[0, span, :], y[1, span, :] = split(dot3(x, inverse, NN))

        fill_panel(z, info, places, c_s, i, p_ref, t_s)
        p = split(t_s[:, :PW])
        high, low = split(t_s[:, PW:] - dot3(p, (z_out[0], z_out[1]), NT))
        p_high[...] = high.reshape(p_high.shape)
        p_low[...] = low.reshape(p_low.shape)
        for n in range(z.half // PW):
            span = slice(n * PW, (n + 1) * PW)
            update = dot3(p, (y[0, span, :], y[1, span, :]), NT)
            for l in range(z.g):
                valid = ((i * z.g + l) * z.rows + info[1]) * B < info[2]
                t_out[l, :, span] = (
                    jnp.where(valid, x_ref[l, :, span], 0.0) - update[l * B : (l + 1) * B]
                )


def pick_kernel(z, info, *refs):
    w0, w1, refs = refs[: z.n0], refs[z.n0 : z.n0 + z.rows], refs[z.n0 + z.rows :]
    late, (_, out, w_s, sems) = refs[: z.fronts], refs[z.fronts :]
    narrow = z.half - KP

    @pl.when(info[0] == 1)
    def _():
        copies = Copies(sems)
        used = z.window_blocks(z.a_first, z.a_count)
        pick = lambda piece: [(l + z.npl, piece(l)) for l in used]
        started = []
        for n, pieces in enumerate((w0, w1)):
            cols = pl.ds(n * PW, PW)
            started += take_rows(
                copies, info[1], gathered(z, pieces), w_s, z.a_first, z.a_count, pick, cols
            )
        for d in range(z.fronts):
            started.append(copies.start(late[d].at[:, pl.ds(0, narrow)], w_s.at[z.narrow_at(d)]))
        copies.wait(started)
        copies.wait([copies.start(w_s, out)])


def final_kernel(z, info, mine, theirs, mine2, theirs2, l0_ref, l1_ref, z_ref, *refs):
    f = z.fronts
    w0, w1, refs = refs[: z.n0], refs[z.n0 : z.n0 + z.rows], refs[z.n0 + z.rows :]
    late, refs = refs[:f], refs[f:]
    x_ref, t_ref, p_high, p_low, out = refs[:5]
    t_s, c_s, w_s, e_s, i_s, s_s, inv, y, places, sems = refs[5:]
    i = pl.program_id(0)

    def add_late(cols):
        for d in range(f):
            at = places[d] - i * z.g

            @pl.when((at >= 0) & (at < z.g))
            def _():
                out[at, :, cols] += e_s[d, :, cols]

    @pl.when(info[0] == 0)
    def _():
        copies = Copies(sems)
        right = pl.ds(KP, z.half - KP)

        @pl.when(i == 0)
        def _():
            started = [
                copies.start(theirs2.at[pl.ds(0, PW), :], w_s.at[pl.ds(0, PW), :]),
                copies.start(mine2.at[pl.ds(0, PW), pl.ds(0, PW)], i_s),
                copies.start(theirs, c_s),
            ]
            started += take_factor(copies, mine, s_s)
            started += [copies.start(theirs2.at[z.narrow_at(d)], e_s.at[d, :, right]) for d in range(f)]
            copies.wait(started)
            read_places(z, c_s, places)
            for n, value in enumerate((s_s[:, :PW], s_s[:, PW:], i_s[...])):
                inv[n, 0], inv[n, 1] = split(value)
            x = split(dot3(split(w_s[:PW, :PW]), (inv[0, 0], inv[0, 1]), NT))
            inv[3, 0], inv[3, 1] = x
            later = split(w_s[:PW, PW:] - dot3(x, (inv[1, 0], inv[1, 1]), NT))
            inv[4, 0], inv[4, 1] = split(dot3(later, (inv[2, 0], inv[2, 1]), NT))

        fill_panel(z, info, places, c_s, i, x_ref, t_s)
        x0 = dot3(split(t_s[:, :PW]), (inv[0, 0], inv[0, 1]), NT)
        x0s = split(x0)
        later = split(t_s[:, PW:] - dot3(x0s, (inv[1, 0], inv[1, 1]), NT))
        x1 = dot3(later, (inv[2, 0], inv[2, 1]), NT)
        update = dot3(x0s, (inv[3, 0], inv[3, 1]), NT) + dot3(split(x1), (inv[4, 0], inv[4, 1]), NT)
        for l in range(z.g):
            span = slice(l * B, (l + 1) * B)
            valid = ((i * z.g + l) * z.rows + info[1]) * B < info[2]
            out[l, :, :PW] = x0[span]
            out[l, :, PW:KP] = x1[span]
            out[l, :, KP:] = jnp.where(valid, x_ref[l, :, KP:], 0.0) - update[span]
        add_late(slice(KP, z.half))

        @pl.when(i == 0)
        def _():
            for l in range(z.npl):
                row = (l * z.rows + info[1]) * B
                out[l, :, PW:] = jnp.zeros((B, z.half - PW), F32)

                @pl.when(row < PW)
                def _():
                    here = pl.ds(pl.multiple_of(row, B), B)
                    copy = pltpu.make_async_copy(l0_ref.at[here], out.at[l, :, pl.ds(0, PW)], sems.at[0])
                    copy.start()
                    copy.wait()

                @pl.when(row >= PW)
                def _():
                    here = pl.ds(pl.multiple_of(row - PW, B), B)
                    piece = (row - PW) // B
                    first = pltpu.make_async_copy(mine.at[piece, pl.ds(0, B), pl.ds(PW, PW)], out.at[l, :, pl.ds(0, PW)], sems.at[0])
                    second = pltpu.make_async_copy(l1_ref.at[here], out.at[l, :, pl.ds(PW, PW)], sems.at[1])
                    first.start()
                    second.start()
                    first.wait()
                    second.wait()

    @pl.when(info[0] == 1)
    def _():
        copies = Copies(sems)

        @pl.when(i == 0)
        def _():
            used = z.window_blocks(z.b_first, z.b_count)
            pick = lambda piece: [(l + z.npl, piece(l)) for l in used]
            started = [copies.start(theirs2.at[pl.ds(0, PW), pl.ds(0, PW)], i_s)]
            started.append(copies.start(z_ref, inv.at[1]))
            started.append(copies.start(mine.at[:, pl.ds(B, EXT - B)], c_s.at[:, pl.ds(B, EXT - B)]))
            for n, pieces in enumerate((w0, w1)):
                cols = pl.ds(n * PW, PW)
                started += take_rows(
                    copies, info[1], gathered(z, pieces), w_s, z.b_first, z.b_count, pick, cols
                )
            right = pl.ds(z.half - KP, z.half)
            arriving = [copies.start(late[d].at[:, right], e_s.at[d]) for d in range(f)]
            copies.wait(started)
            read_places(z, c_s, places)
            inv[0, 0], inv[0, 1] = split(i_s[...])
            inverse = (inv[0, 0], inv[0, 1])
            for n in range(z.half // PW):
                span = slice(n * PW, (n + 1) * PW)
                w = w_s[span, PW:] - dot3(split(w_s[span, :PW]), (inv[1, 0], inv[1, 1]), NT)
                x = split(dot3(split(w), inverse, NT))
                y[0, span, :], y[1, span, :] = split(dot3(x, inverse, NN))
            copies.wait(arriving)

        p = (p_high[...].reshape(z.g * B, PW), p_low[...].reshape(z.g * B, PW))
        for n in range(z.half // PW):
            span = slice(n * PW, (n + 1) * PW)
            update = dot3(p, (y[0, span, :], y[1, span, :]), NT)
            for l in range(z.g):
                out[l, :, span] = t_ref[l, :, span] - update[l * B : (l + 1) * B]
        add_late(slice(0, z.half))

        @pl.when(i == 0)
        def _():
            for l in range(z.npl):
                out[l] = jnp.zeros((B, z.half), F32)


ANY = pl.BlockSpec(memory_space=pl.ANY)
WHOLE = pl.BlockSpec(memory_space=pltpu.VMEM)
SCALARS = pl.BlockSpec(memory_space=pltpu.SMEM)
PARAMS = pltpu.CompilerParams(vmem_limit_bytes=VMEM_LIMIT)


def shape(*dims, dtype=F32):
    return jax.ShapeDtypeStruct(dims, dtype)


def after(value, *others):
    return lax.optimization_barrier((value, *others))[0]


def on_device(front_matrix, front_sizes, contrib, dest_front, dest_local):
    fronts = lax.axis_size("front")
    rows = lax.axis_size("row")
    front_here = lax.axis_index("front")
    row_here = lax.axis_index("row")
    col_here = lax.axis_index("col")
    matrix = front_matrix[0]
    blocks = contrib[0]
    blocks_here, _, half = matrix.shape
    z = Sizes(rows, fronts, blocks.shape[0], blocks_here, half)

    def from_rows(x, core):
        return [x] + [along_rows(x, k, core) for k in range(1, rows)]

    def along_rows(x, k, core):
        pairs = [(r * 2 + core, (r ^ k) * 2 + core) for r in range(rows)]
        return lax.ppermute(x, ("row", "col"), pairs)

    def along_fronts(x, d, source, target):
        pairs = [(f * 2 + source, (f + d) % fronts * 2 + target) for f in range(fronts)]
        return lax.ppermute(x, ("front", "col"), pairs)

    def to_other(x):
        return lax.ppermute(x, "col", [(0, 1)])

    def swap(x):
        return lax.ppermute(x, "col", [(0, 1), (1, 0)])

    info = jnp.concatenate(
        [
            jnp.stack([col_here, row_here]).astype(jnp.int32),
            front_sizes,
            front_here.astype(jnp.int32)[None],
        ]
    )
    dest = jnp.concatenate([dest_front[0, :, 0], dest_local[0, :, 0]])

    q0 = matrix[0, :, :PW]
    if z.npl == 2:
        pivot0 = from_rows(q0, 0)
    other_blocks = to_other(blocks)
    other = to_other(after(matrix, other_blocks))
    pivot1 = from_rows(matrix[z.npl - 1, :, :KP], 0)
    if z.npl != 2:
        pivot0 = pivot1

    factor_scratch = [
        pltpu.VMEM((PW, PW), F32),
        pltpu.VMEM((PW, 2 * PW), F32),
        pltpu.VMEM((B, B), F32),
        pltpu.VMEM((B, B), F32),
    ]
    l0, i0 = pl.pallas_call(
        functools.partial(factor0_kernel, z),
        out_shape=[shape(PW, PW)] * 2,
        in_specs=[SCALARS] + [ANY] * rows,
        out_specs=[WHOLE] * 2,
        scratch_shapes=factor_scratch + [pltpu.SemaphoreType.DMA((rows,))],
        compiler_params=PARAMS,
        name="factor0",
    )(info, *pivot0)
    packed = pl.pallas_call(
        functools.partial(middle_kernel, z),
        out_shape=shape(fronts, EXT, KP),
        in_specs=[SCALARS] + [ANY] * (rows + 1),
        out_specs=ANY,
        scratch_shapes=[
            pltpu.VMEM((PW, PW), F32),
            pltpu.VMEM((PW, 2 * PW), F32),
            pltpu.SemaphoreType.DMA((rows + NB + 1,)),
        ],
        compiler_params=PARAMS,
        name="middle",
    )(info, i0, *pivot1)

    refs = pl.pallas_call(
        functools.partial(sort_kernel, z),
        out_shape=[shape(EXT, KP)] * fronts + [shape(B, 2 * half - KP)] * fronts,
        in_specs=[SCALARS] * 2 + [ANY] * 2,
        out_specs=[ANY] * (2 * fronts),
        scratch_shapes=[
            pltpu.VMEM((fronts, EXT, KP), F32),
            pltpu.VMEM((fronts, B, 2 * half - KP), F32),
            pltpu.SemaphoreType.DMA((5 * fronts,)),
        ],
        compiler_params=PARAMS,
        name="sort",
    )(info, dest, after(other_blocks, packed), blocks)
    panel, late = list(refs[:fronts]), list(refs[fronts:])
    panel = panel[:1] + [along_fronts(x, d + 1, 1, 1) for d, x in enumerate(panel[1:])]
    h0, h1, mine = pl.pallas_call(
        functools.partial(window_kernel, z),
        out_shape=[shape(z.windows, B, PW)] * 2 + [shape(fronts, EXT, KP)],
        in_specs=[SCALARS] + [ANY] * (fronts + 2),
        out_specs=[ANY] * 3,
        input_output_aliases={2: 2},
        scratch_shapes=[
            pltpu.VMEM((z.windows, B, KP), F32),
            pltpu.VMEM((fronts, EXT, KP), F32),
            pltpu.SMEM((fronts,), jnp.int32),
            pltpu.SemaphoreType.DMA((fronts + 4,)),
        ],
        compiler_params=PARAMS,
        name="window",
    )(info, other, packed, *panel)
    if z.n0 == rows:
        w0 = from_rows(h0, 1)
    else:
        middle = z.windows // 2
        sides = [along_rows(h0, 1, 1), along_rows(h0, 2, 1)]
        across = [along_rows(sides[0][:middle], 2, 1), along_rows(sides[1][middle:], 1, 1)]
        w0 = [h0, *sides, *across]
    late = late[:1] + [along_fronts(after(x, h0), d + 1, 1, 1) for d, x in enumerate(late[1:])]
    theirs = swap(after(mine, *w0))
    w1 = from_rows(after(h1, *w0), 1)

    def tile(width, core):
        return pl.BlockSpec((z.g, B, width), lambda i, s: (jnp.where(s[0] == core, i, 0), 0, 0))

    both = pltpu.VMEM((2, PW, PW), BF16)
    rest = half - KP + -(-fronts * (half - KP) // KP) * B
    l1, mine2, trailing, p_high, p_low, z_pair = pl.pallas_call(
        functools.partial(both_kernel, z),
        out_shape=[
            shape(PW, PW),
            shape(rest, KP),
            shape(blocks_here, B, half),
            shape(blocks_here, B, PW, dtype=BF16),
            shape(blocks_here, B, PW, dtype=BF16),
            shape(2, PW, PW, dtype=BF16),
        ],
        grid_spec=pltpu.PrefetchScalarGridSpec(
            num_scalar_prefetch=1,
            grid=(z.tiles,),
            in_specs=[ANY] * (2 + rows + z.n0) + [tile(KP, 1), tile(half, 1)],
            out_specs=[WHOLE, ANY, tile(half, 1), tile(PW, 1), tile(PW, 1), WHOLE],
            scratch_shapes=factor_scratch[:1]
            + [pltpu.VMEM((PW, 2 * PW), F32), pltpu.VMEM((PW, PW), F32)]
            + factor_scratch[1:]
            + [
                pltpu.VMEM((half, PW), F32),
                pltpu.VMEM((z.g * B, KP), F32),
                pltpu.VMEM((fronts, EXT, KP), F32),
                both,
                pltpu.VMEM((2, half, PW), BF16),
                pltpu.SMEM((fronts,), jnp.int32),
                pltpu.SemaphoreType.DMA((rows * z.windows + NB + 2,)),
            ],
        ),
        compiler_params=PARAMS,
        name="factor1_update0",
    )(info, mine, theirs, *pivot1, *w0, other, matrix)

    mine2 = pl.pallas_call(
        functools.partial(pick_kernel, z),
        out_shape=shape(rest, KP),
        in_specs=[SCALARS] + [ANY] * (z.n0 + rows + fronts + 1),
        out_specs=ANY,
        scratch_shapes=[
            pltpu.VMEM((rest, KP), F32),
            pltpu.SemaphoreType.DMA((2 * rows * z.windows + fronts + 1,)),
        ],
        input_output_aliases={1 + z.n0 + rows + fronts: 0},
        compiler_params=PARAMS,
        name="pick",
    )(info, *w0, *w1, *late, mine2)
    theirs2 = swap(mine2)

    out = pl.pallas_call(
        functools.partial(final_kernel, z),
        out_shape=shape(blocks_here, B, half),
        grid_spec=pltpu.PrefetchScalarGridSpec(
            num_scalar_prefetch=1,
            grid=(z.tiles,),
            in_specs=[ANY] * (7 + z.n0 + rows + fronts)
            + [tile(half, 0), tile(half, 1), tile(PW, 1), tile(PW, 1)],
            out_specs=pl.BlockSpec((z.g, B, half), lambda i, s: (i, 0, 0)),
            scratch_shapes=[
                pltpu.VMEM((z.g * B, KP), F32),
                pltpu.VMEM((fronts, EXT, KP), F32),
                pltpu.VMEM((half, KP), F32),
                pltpu.VMEM((fronts, B, half), F32),
                pltpu.VMEM((PW, PW), F32),
                pltpu.VMEM((PW, 2 * PW), F32),
                pltpu.VMEM((5, 2, PW, PW), BF16),
                pltpu.VMEM((2, half, PW), BF16),
                pltpu.SMEM((fronts,), jnp.int32),
                pltpu.SemaphoreType.DMA((2 * rows * z.windows + fronts + 8,)),
            ],
        ),
        compiler_params=PARAMS,
        name="final",
    )(info, mine, theirs, mine2, theirs2, l0, l1, z_pair, *w0, *w1, *late, matrix, trailing, p_high, p_low)
    return out[None]


def solution(mesh):
    return jax.shard_map(
        on_device,
        mesh=mesh,
        in_specs=(
            P("front", None, "row", "col"),
            P("front"),
            P("front", None, "row", "col"),
            P("front", None, "row"),
            P("front", None, "row"),
        ),
        out_specs=P("front", None, "row", "col"),
        check_vma=False,
    )
```

```python
import functools

import jax
import jax.numpy as jnp
from jax import lax
from jax.experimental import pallas as pl
from jax.experimental.pallas import tpu as pltpu
from jax.sharding import PartitionSpec as P

PW = 512
NPANEL = 2
B = 128
KP = PW * NPANEL
NB = PW // B
EXT = B + 8
NT = ((1,), (1,))
NN = ((1,), (0,))
TN = ((0,), (0,))
F32 = jnp.float32
BF16 = jnp.bfloat16
VMEM_LIMIT = 56 * 2**20


def split(x):
    high = x.astype(BF16)
    return high, (x - high.astype(F32)).astype(BF16)


def dot3(a, b, dims):
    def one(u, v):
        return lax.dot_general(u, v, (dims, ((), ())), preferred_element_type=F32)

    return one(a[0], b[0]) + (one(a[0], b[1]) + one(a[1], b[0]))


def dot6(a, b, dims):
    return lax.dot_general(
        a, b, (dims, ((), ())), precision=lax.Precision.HIGHEST, preferred_element_type=F32
    )


def over_lanes(group, lane):
    return jnp.broadcast_to(group[:, lane : lane + 1], group.shape)


def over_rows(group, row):
    return jnp.broadcast_to(group[row : row + 1, :], group.shape)


def factor_block(s_ref, v_ref, u_ref):
    sub = lax.broadcasted_iota(jnp.int32, (8, B), 0)
    lane = lax.broadcasted_iota(jnp.int32, (8, B), 1)
    n = B // 8
    left = [s_ref[8 * g : 8 * g + 8, :] for g in range(n)]
    right = [jnp.where(lane == sub + 8 * g, 1.0, 0.0).astype(F32) for g in range(n)]
    for b in range(n):
        cols = [[over_lanes(left[g], 8 * b + j) for j in range(8)] for g in range(b, n)]
        scale = jnp.ones((8, B), F32)
        for j in range(8):
            pivot = over_rows(cols[0][j], j)
            inv = 1.0 / pivot
            lrow = over_rows(left[b], j)
            rrow = over_rows(right[b], j)
            krow = [over_rows(cols[0][k], j) if k > j else None for k in range(8)]
            scale = jnp.where(sub == j, lax.rsqrt(pivot), scale)
            for g in range(b, n):
                f = cols[g - b][j] * inv
                if g == b:
                    f = jnp.where(sub > j, f, 0.0)
                for k in range(j + 1, 8):
                    cols[g - b][k] = cols[g - b][k] - f * krow[k]
                left[g] = left[g] - f * lrow
                right[g] = right[g] - f * rrow
        u_ref[8 * b : 8 * b + 8, :] = jnp.where(lane >= sub + 8 * b, left[b] * scale, 0.0)
        v_ref[8 * b : 8 * b + 8, :] = right[b] * scale


def panel_factor(m_ref, u_ref, v_ref):
    def body(k, _):
        c = pl.multiple_of(k * B, B)
        factor_block(m_ref.at[pl.ds(c, B), pl.ds(c, B)], v_ref, u_ref)
        row = dot6(v_ref[...], m_ref[pl.ds(c, B), :], NN)
        m_ref[pl.ds(c, B), :] = row
        m_ref[pl.ds(c, B), pl.ds(c, B)] = u_ref[...]
        for i in range(1, NB):

            @pl.when(i > k)
            def _():
                up = m_ref[pl.ds(c, B), i * B : (i + 1) * B]
                rows = slice(i * B, (i + 1) * B)
                m_ref[rows, :] = m_ref[rows, :] - dot6(up, row, TN)

        return 0

    lax.fori_loop(0, NB, body, 0)


def load_symmetric(a_ref, m_ref, col):
    r = lax.broadcasted_iota(jnp.int32, (B, B), 0)
    c = lax.broadcasted_iota(jnp.int32, (B, B), 1)
    for i in range(NB):
        for j in range(NB):
            here = (slice(i * B, (i + 1) * B), slice(PW + j * B, PW + (j + 1) * B))
            m_ref[here] = jnp.where(r == c, 1.0, 0.0) if i == j else jnp.zeros((B, B), F32)
            if j > i:
                continue
            block = a_ref[i * B : (i + 1) * B, col + j * B : col + (j + 1) * B]
            if i == j:
                block = jnp.where(r >= c, block, block.T)
                m_ref[i * B : (i + 1) * B, i * B : (i + 1) * B] = block
            else:
                m_ref[i * B : (i + 1) * B, j * B : (j + 1) * B] = block
                m_ref[j * B : (j + 1) * B, i * B : (i + 1) * B] = block.T


def store_factor(m_ref, l_ref, i_ref):
    for i in range(NB):
        for j in range(NB):
            here = (slice(i * B, (i + 1) * B), slice(j * B, (j + 1) * B))
            if j <= i:
                l_ref[here] = m_ref[j * B : (j + 1) * B, i * B : (i + 1) * B].T
            else:
                l_ref[here] = jnp.zeros((B, B), F32)
    i_ref[...] = m_ref[:, PW:]


class Copies:
    def __init__(self, sems):
        self.sems, self.count = sems, 0

    def start(self, src, dst, when=None):
        copy = pltpu.make_async_copy(src, dst, self.sems.at[self.count])
        self.count += 1
        if when is None:
            copy.start()
        else:
            pl.when(when)(copy.start)
        return copy, when

    @staticmethod
    def wait(started):
        for copy, when in started:
            if when is None:
                copy.wait()
            else:
                pl.when(when)(copy.wait)


def take_rows(copies, me, pieces, dst, first, count, pick, cols):
    started = []
    rows = len(pieces)
    for k, piece in enumerate(pieces):
        for l, src in pick(piece):
            at = (me ^ k) + l * rows - first
            low, high = l * rows - first, l * rows - first + rows - 1
            inside = None if low >= 0 and high < count else (at >= 0) & (at < count)
            clipped = at if inside is None else jnp.clip(at, 0, count - 1)
            here = pl.ds(pl.multiple_of(clipped * B, B), B)
            started.append(copies.start(src, dst.at[here, cols], inside))
    return started


class Sizes:
    def __init__(self, rows, fronts, per_device, blocks_here, half):
        self.rows, self.fronts, self.kb = rows, fronts, per_device
        self.blocks, self.half = blocks_here, half
        self.npl = KP // (rows * B)
        self.g = max(1, blocks_here // 6)
        self.tiles = blocks_here // self.g
        self.windows = 2 * half // (rows * B) - self.npl
        self.pivot_first = 0 if self.npl == 2 else NB
        self.pivot_cols = PW if self.npl == 2 else 0
        self.gathers = rows + 1 if rows == 4 and self.windows % 2 == 0 else rows
        self.a_first = KP // B
        self.a_count = (half - KP) // B
        self.b_first = half // B
        self.b_count = half // B

    def narrow_at(self, d):
        width = self.half - KP
        per = KP // width
        return (pl.ds(self.half - KP + d // per * B, B), pl.ds(d % per * width, width))

    def window_blocks(self, first, count):
        return range(first // self.rows - self.npl, (first + count - 1) // self.rows + 1 - self.npl)


def gathered(z, refs):
    if len(refs) == z.rows:
        return [lambda l, ref=ref: ref.at[l] for ref in refs]
    half = z.windows // 2
    whole, (first, second) = refs[: z.rows - 1], refs[z.rows - 1 :]
    across = lambda l: first.at[l] if l < half else second.at[l - half]
    return [lambda l, ref=ref: ref.at[l] for ref in whole] + [across]


def route(z, info, d):
    front = lax.rem(info[3] + d, z.fronts)
    slot, place = jnp.int32(0), jnp.int32(-1)
    for k in range(z.kb):
        hit = info[4 + k] == front
        slot = jnp.where(hit, k, slot)
        place = jnp.where(hit, info[4 + z.kb + k], place)
    return slot, place


def read_places(z, blocks, places, first=B):
    for d in range(z.fronts):
        places[d] = jnp.max(blocks[d, first : first + EXT - B, :B]).astype(jnp.int32)


def factor0_kernel(z, info, *refs):
    pieces, (l_out, i_out, a_ref, m_ref, u_ref, v_ref, sems) = refs[: z.rows], refs[z.rows :]

    @pl.when(info[0] == 0)
    def _():
        copies = Copies(sems)
        pick = lambda piece: [(0, piece.at[:, pl.ds(0, PW)])]
        copies.wait(take_rows(copies, info[1], pieces, a_ref, 0, NB, pick, slice(None)))
        load_symmetric(a_ref, m_ref, 0)
        panel_factor(m_ref, u_ref, v_ref)
        store_factor(m_ref, l_out, i_out)


def middle_kernel(z, info, i0_ref, *refs):
    pieces, (out, a_ref, f_s, sems) = refs[: z.rows], refs[z.rows :]

    @pl.when(info[0] == 0)
    def _():
        copies = Copies(sems)
        pick = lambda piece: [(0, piece.at[:, pl.ds(z.pivot_cols, PW)])]
        started = take_rows(copies, info[1], pieces, a_ref, z.pivot_first, NB, pick, slice(None))
        started.append(copies.start(i0_ref, f_s.at[:, pl.ds(0, PW)]))
        copies.wait(started)
        f_s[:, PW:] = dot6(a_ref[...], f_s[:, :PW], NT)
        copies.wait(
            [copies.start(f_s.at[pl.ds(n * B, B)], out.at[n, pl.ds(0, B)]) for n in range(NB)]
        )


def take_factor(copies, packed, f_s):
    return [copies.start(packed.at[n, pl.ds(0, B)], f_s.at[pl.ds(n * B, B)]) for n in range(NB)]


def sort_kernel(z, info, first, second, *refs):
    f = z.fronts
    panel, late = refs[:f], refs[f : 2 * f]
    c_s, e_s, sems = refs[2 * f :]
    narrow = z.half - KP

    @pl.when(info[0] == 1)
    def _():
        copies = Copies(sems)
        routes = [route(z, info, d) for d in range(f)]
        order = list(range(1, f)) + [0]
        reads = {}
        for d in order:
            slot, place = routes[d]
            c_s[d, B:EXT, :B] = jnp.full((EXT - B, B), place.astype(F32))
            reads[d] = copies.start(first.at[slot, :, pl.ds(0, KP)], c_s.at[d, pl.ds(0, B)])
        more = []
        for d in order:
            slot = routes[d][0]
            more.append(
                copies.start(first.at[slot, :, pl.ds(KP, narrow)], e_s.at[d, :, pl.ds(0, narrow)])
            )
            more.append(copies.start(second.at[slot], e_s.at[d, :, pl.ds(narrow, z.half)]))
        writes = []
        for d in order:
            copies.wait([reads[d]])
            writes.append(copies.start(c_s.at[d], panel[d]))
        for n, d in enumerate(order):
            copies.wait(more[2 * n : 2 * n + 2])
            writes.append(copies.start(e_s.at[d], late[d]))
        copies.wait(writes)


def window_kernel(z, info, raw, _, *refs):
    f = z.fronts
    panel, (window, back), (t_ref, c_ref, places, sems) = refs[:f], refs[f : f + 2], refs[f + 2 :]

    @pl.when(info[0] == 1)
    def _():
        copies = Copies(sems)
        started = [copies.start(raw, t_ref)]
        started += [copies.start(panel[d], c_ref.at[d]) for d in range(f)]
        copies.wait(started)
        later = [copies.start(c_ref, back)]
        read_places(z, c_ref, places)
        for d in range(f):
            place = places[d] - z.npl

            @pl.when((place >= 0) & (place < z.windows))
            def _():
                t_ref[place] += c_ref[d, :B]

        later.append(copies.start(t_ref, window))
        copies.wait(later)


def fill_panel(z, info, places, blocks, i, p_ref, t_ref):
    for l in range(z.g):
        lb = i * z.g + l
        valid = (lb * z.rows + info[1]) * B < info[2]
        t_ref[l * B : (l + 1) * B, :] = jnp.where(valid, p_ref[l, :, :KP], 0.0)
    for d in range(z.fronts):
        at = places[d] - i * z.g

        @pl.when((at >= 0) & (at < z.g))
        def _():
            here = pl.ds(pl.multiple_of(at * B, B), B)
            t_ref[here, :] += blocks[d, :B]


def factor1_kernel(z, info, mine, *refs):
    pieces, (l_out, i_out, a_ref, f_s, m_ref, u_ref, v_ref, sems) = refs[: z.rows], refs[z.rows :]

    @pl.when(info[0] == 0)
    def _():
        copies = Copies(sems)
        pick = lambda piece: [(0, piece.at[:, pl.ds(z.pivot_cols + PW, PW)])]
        started = take_rows(copies, info[1], pieces, a_ref, z.pivot_first, NB, pick, slice(None))
        started += take_factor(copies, mine, f_s)
        copies.wait(started)
        load_symmetric(a_ref, m_ref, 0)
        m_ref[:, :PW] = m_ref[:, :PW] - dot6(f_s[:, PW:], f_s[:, PW:], NT)
        panel_factor(m_ref, u_ref, v_ref)
        store_factor(m_ref, l_out, i_out)


def panel_kernel(z, info, mine, theirs, p_ref, p_high, p_low, z_out, t_s, c_s, f_s, places, sems):
    i = pl.program_id(0)

    @pl.when(info[0] == 1)
    def _():
        @pl.when(i == 0)
        def _():
            copies = Copies(sems)
            started = take_factor(copies, theirs, f_s)
            started.append(copies.start(mine, c_s))
            copies.wait(started)
            read_places(z, c_s, places)
            product = dot3(split(f_s[:, PW:]), split(f_s[:, :PW]), NN)
            z_out[0], z_out[1] = split(product)

        fill_panel(z, info, places, c_s, i, p_ref, t_s)
        p = split(t_s[:, :PW])
        later = split(t_s[:, PW:] - dot3(p, (z_out[0], z_out[1]), NT))
        for out, first, second in ((p_high, p[0], later[0]), (p_low, p[1], later[1])):
            out[:, :, :PW] = first.reshape(z.g, B, PW)
            out[:, :, PW:] = second.reshape(z.g, B, PW)


def each_chunk(z, body):
    def step(n, _):
        body(pl.ds(pl.multiple_of(n * PW, PW), PW))
        return 0

    lax.fori_loop(0, z.half // PW, step, 0)


def window_solve_kernel(z, info, theirs, z_ref, *refs):
    w, refs = gathered(z, refs[: z.gathers]), refs[z.gathers :]
    w_out, y_out, w_s, f_s, inv, y, sems = refs

    @pl.when(info[0] == 1)
    def _():
        copies = Copies(sems)
        used = z.window_blocks(z.b_first, z.b_count)
        pick = lambda piece: [(l + z.npl, piece(l)) for l in used]
        started = take_factor(copies, theirs, f_s)
        started.append(copies.start(z_ref, inv.at[1]))
        started += take_rows(copies, info[1], w, w_s, z.b_first, z.b_count, pick, slice(None))
        copies.wait(started)
        inv[0, 0], inv[0, 1] = split(f_s[:, :PW])

        def project(span):
            inverse = (inv[0, 0], inv[0, 1])
            first = split(w_s[span, :PW])
            x = split(dot3(first, inverse, NT))
            y[0, span, :], y[1, span, :] = split(dot3(x, inverse, NN))
            w_s[span, PW:] = w_s[span, PW:] - dot3(first, (inv[1, 0], inv[1, 1]), NT)

        each_chunk(z, project)
        copies.wait(
            [copies.start(w_s.at[:, pl.ds(PW, PW)], w_out), copies.start(y, y_out)]
        )


def pick_kernel(z, info, *refs):
    w, refs = gathered(z, refs[: z.gathers]), refs[z.gathers :]
    late, (out, w_s, sems) = refs[: z.fronts], refs[z.fronts :]
    narrow = z.half - KP

    @pl.when(info[0] == 1)
    def _():
        copies = Copies(sems)
        used = z.window_blocks(z.a_first, z.a_count)
        pick = lambda piece: [(l + z.npl, piece(l)) for l in used]
        started = take_rows(copies, info[1], w, w_s, z.a_first, z.a_count, pick, slice(None))
        for d in range(z.fronts):
            started.append(copies.start(late[d].at[:, pl.ds(0, narrow)], w_s.at[z.narrow_at(d)]))
        copies.wait(started)
        copies.wait([copies.start(w_s, out)])


def final_kernel(z, info, mine, theirs, rest, i1_ref, i1r_ref, l0_ref, l1_ref, w_ref, y_ref, *refs):
    f = z.fronts
    late, (x_ref, p_high, p_low, out), refs = refs[:f], refs[f : f + 4], refs[f + 4 :]
    t_s, c_s, w_s, e_s, i_s, s_s, inv, y, places, sems = refs
    i = pl.program_id(0)

    def add_late(cols):
        for d in range(f):
            at = places[d] - i * z.g

            @pl.when((at >= 0) & (at < z.g))
            def _():
                out[at, :, cols] += e_s[d, :, cols]

    def valid(l):
        return ((i * z.g + l) * z.rows + info[1]) * B < info[2]

    @pl.when(info[0] == 0)
    def _():
        copies = Copies(sems)

        @pl.when(i == 0)
        def _():
            started = [
                copies.start(rest.at[pl.ds(0, PW), pl.ds(0, PW)], w_s.at[0]),
                copies.start(rest.at[pl.ds(0, PW), pl.ds(PW, PW)], w_s.at[1]),
                copies.start(i1_ref, i_s),
                copies.start(theirs, c_s),
            ]
            started += take_factor(copies, mine, s_s)
            right = pl.ds(KP, z.half - KP)
            arriving = [copies.start(rest.at[z.narrow_at(d)], e_s.at[d, :, right]) for d in range(f)]
            copies.wait(started)
            read_places(z, c_s, places)
            for n, value in enumerate((s_s[:, :PW], s_s[:, PW:], i_s[...])):
                inv[n, 0], inv[n, 1] = split(value)
            x = split(dot3(split(w_s[0]), (inv[0, 0], inv[0, 1]), NT))
            inv[3, 0], inv[3, 1] = x
            later = split(w_s[1] - dot3(x, (inv[1, 0], inv[1, 1]), NT))
            inv[4, 0], inv[4, 1] = split(dot3(later, (inv[2, 0], inv[2, 1]), NT))
            copies.wait(arriving)

        fill_panel(z, info, places, c_s, i, x_ref, t_s)
        x0 = dot3(split(t_s[:, :PW]), (inv[0, 0], inv[0, 1]), NT)
        x0s = split(x0)
        later = split(t_s[:, PW:] - dot3(x0s, (inv[1, 0], inv[1, 1]), NT))
        x1 = dot3(later, (inv[2, 0], inv[2, 1]), NT)
        update = dot3(x0s, (inv[3, 0], inv[3, 1]), NT) + dot3(split(x1), (inv[4, 0], inv[4, 1]), NT)
        for l in range(z.g):
            span = slice(l * B, (l + 1) * B)
            out[l, :, :PW] = x0[span]
            out[l, :, PW:KP] = x1[span]
            out[l, :, KP:] = jnp.where(valid(l), x_ref[l, :, KP:], 0.0) - update[span]
        add_late(slice(KP, z.half))

        @pl.when(i == 0)
        def _():
            for l in range(z.npl):
                row = (l * z.rows + info[1]) * B
                out[l, :, PW:] = jnp.zeros((B, z.half - PW), F32)

                @pl.when(row < PW)
                def _():
                    here = pl.ds(pl.multiple_of(row, B), B)
                    copy = pltpu.make_async_copy(l0_ref.at[here], out.at[l, :, pl.ds(0, PW)], sems.at[0])
                    copy.start()
                    copy.wait()

                @pl.when(row >= PW)
                def _():
                    here = pl.ds(pl.multiple_of(row - PW, B), B)
                    out[l, :, :PW] = s_s[here, PW:]
                    copy = pltpu.make_async_copy(l1_ref.at[here], out.at[l, :, pl.ds(PW, PW)], sems.at[0])
                    copy.start()
                    copy.wait()

    @pl.when(info[0] == 1)
    def _():
        copies = Copies(sems)

        @pl.when(i == 0)
        def _():
            started = [
                copies.start(i1r_ref, i_s),
                copies.start(mine.at[:, pl.ds(B, EXT - B)], c_s.at[:, pl.ds(B, EXT - B)]),
            ]
            for n in range(z.half // PW):
                started.append(copies.start(w_ref.at[pl.ds(n * PW, PW)], w_s.at[n]))
            arriving = [copies.start(y_ref, y.at[0])]
            right = pl.ds(z.half - KP, z.half)
            arriving += [copies.start(late[d].at[:, right], e_s.at[d]) for d in range(f)]
            copies.wait(started)
            read_places(z, c_s, places)
            inverse = split(i_s[...])
            inv[0, 0], inv[0, 1] = inverse

            def project(n, _):
                inverse = (inv[0, 0], inv[0, 1])
                span = pl.ds(pl.multiple_of(n * PW, PW), PW)
                x = split(dot3(split(w_s[n]), inverse, NT))
                y[1, 0, span, :], y[1, 1, span, :] = split(dot3(x, inverse, NN))
                return 0

            lax.fori_loop(0, z.half // PW, project, 0)
            copies.wait(arriving)

        p0 = tuple(p[:, :, :PW].reshape(z.g * B, PW) for p in (p_high, p_low))
        p1 = tuple(p[:, :, PW:].reshape(z.g * B, PW) for p in (p_high, p_low))

        def subtract(span):
            update = dot3(p0, (y[0, 0, span, :], y[0, 1, span, :]), NT)
            update = update + dot3(p1, (y[1, 0, span, :], y[1, 1, span, :]), NT)
            for l in range(z.g):
                present = jnp.where(valid(l), x_ref[l, :, span], 0.0)
                out[l, :, span] = present - update[l * B : (l + 1) * B]

        for n in range(z.half // PW):
            subtract(slice(n * PW, (n + 1) * PW))
        add_late(slice(0, z.half))

        @pl.when(i == 0)
        def _():
            for l in range(z.npl):
                out[l] = jnp.zeros((B, z.half), F32)


ANY = pl.BlockSpec(memory_space=pl.ANY)
WHOLE = pl.BlockSpec(memory_space=pltpu.VMEM)
SCALARS = pl.BlockSpec(memory_space=pltpu.SMEM)
PARAMS = pltpu.CompilerParams(vmem_limit_bytes=VMEM_LIMIT)
SHORT = pl.CostEstimate(flops=1, bytes_accessed=1, transcendentals=0)


def shape(*dims, dtype=F32):
    return jax.ShapeDtypeStruct(dims, dtype)


def after(value, *others):
    return lax.optimization_barrier((value, *others))[0]


def on_device(front_matrix, front_sizes, contrib, dest_front, dest_local):
    fronts = lax.axis_size("front")
    rows = lax.axis_size("row")
    front_here = lax.axis_index("front")
    row_here = lax.axis_index("row")
    col_here = lax.axis_index("col")
    matrix = front_matrix[0]
    blocks = contrib[0]
    blocks_here, _, half = matrix.shape
    z = Sizes(rows, fronts, blocks.shape[0], blocks_here, half)

    def from_rows(x, core):
        return [x] + [along_rows(x, k, core) for k in range(1, rows)]

    def along_rows(x, k, core):
        pairs = [(r * 2 + core, (r ^ k) * 2 + core) for r in range(rows)]
        return lax.ppermute(x, ("row", "col"), pairs)

    def along_fronts(x, d, source, target):
        pairs = [(f * 2 + source, (f + d) % fronts * 2 + target) for f in range(fronts)]
        return lax.ppermute(x, ("front", "col"), pairs)

    def to_other(x):
        return lax.ppermute(x, "col", [(0, 1)])

    def swap(x):
        return lax.ppermute(x, "col", [(0, 1), (1, 0)])

    def from_other(x):
        return lax.ppermute(x, "col", [(1, 0)])

    info = jnp.concatenate(
        [
            jnp.stack([col_here, row_here]).astype(jnp.int32),
            front_sizes,
            front_here.astype(jnp.int32)[None],
            dest_front[0, :, 0],
            dest_local[0, :, 0],
        ]
    )
    other_blocks = to_other(blocks)
    pivot = matrix[z.npl - 1, :, :KP]
    if z.npl == 2:
        pivot = jnp.concatenate([matrix[0, :, :PW], pivot], axis=1)
    pivots = from_rows(pivot, 0)
    raw = to_other(after(matrix, pivot)[z.npl : z.npl + z.windows, :, :KP])
    other = to_other(after(matrix, other_blocks, *pivots, raw))

    factor_scratch = [
        pltpu.VMEM((PW, PW), F32),
        pltpu.VMEM((PW, 2 * PW), F32),
        pltpu.VMEM((B, B), F32),
        pltpu.VMEM((B, B), F32),
    ]
    l0, i0 = pl.pallas_call(
        functools.partial(factor0_kernel, z),
        out_shape=[shape(PW, PW)] * 2,
        in_specs=[SCALARS] + [ANY] * rows,
        out_specs=[WHOLE] * 2,
        scratch_shapes=factor_scratch + [pltpu.SemaphoreType.DMA((rows,))],
        compiler_params=PARAMS,
        cost_estimate=SHORT,
        name="factor0",
    )(info, *pivots)
    packed = pl.pallas_call(
        functools.partial(middle_kernel, z),
        out_shape=shape(fronts, EXT, KP),
        in_specs=[SCALARS] + [ANY] * (rows + 1),
        out_specs=ANY,
        scratch_shapes=[
            pltpu.VMEM((PW, PW), F32),
            pltpu.VMEM((PW, 2 * PW), F32),
            pltpu.SemaphoreType.DMA((rows + NB + 1,)),
        ],
        compiler_params=PARAMS,
        cost_estimate=SHORT,
        name="middle",
    )(info, i0, *pivots)

    refs = pl.pallas_call(
        functools.partial(sort_kernel, z),
        out_shape=[shape(EXT, KP)] * fronts + [shape(B, 2 * half - KP)] * fronts,
        in_specs=[SCALARS] + [ANY] * 2,
        out_specs=[ANY] * (2 * fronts),
        scratch_shapes=[
            pltpu.VMEM((fronts, EXT, KP), F32),
            pltpu.VMEM((fronts, B, 2 * half - KP), F32),
            pltpu.SemaphoreType.DMA((5 * fronts,)),
        ],
        compiler_params=PARAMS,
        cost_estimate=SHORT,
        name="sort",
    )(info, other_blocks, blocks)
    panel, late = list(refs[:fronts]), list(refs[fronts:])
    panel = panel[:1] + [along_fronts(x, d + 1, 1, 1) for d, x in enumerate(panel[1:])]
    window, mine = pl.pallas_call(
        functools.partial(window_kernel, z),
        out_shape=[shape(z.windows, B, KP), shape(fronts, EXT, KP)],
        in_specs=[SCALARS] + [ANY] * (fronts + 2),
        out_specs=[ANY] * 2,
        input_output_aliases={2: 1},
        scratch_shapes=[
            pltpu.VMEM((z.windows, B, KP), F32),
            pltpu.VMEM((fronts, EXT, KP), F32),
            pltpu.SMEM((fronts,), jnp.int32),
            pltpu.SemaphoreType.DMA((fronts + 4,)),
        ],
        compiler_params=PARAMS,
        cost_estimate=SHORT,
        name="window",
    )(info, raw, packed, *panel)
    late = late[:1] + [along_fronts(after(x, window), d + 1, 1, 1) for d, x in enumerate(late[1:])]
    if z.gathers == rows:
        windows = from_rows(window, 1)
        theirs = swap(mine)
    else:
        middle = z.windows // 2
        sides = [along_rows(window, 1, 1), along_rows(window, 2, 1)]
        windows = [window, *sides]
        theirs = swap(after(mine, *sides, late[1], late[-1]))
        windows += [along_rows(sides[0][:middle], 2, 1), along_rows(sides[1][middle:], 1, 1)]

    def tile(width, core, part=0):
        return pl.BlockSpec((z.g, B, width), lambda i, s: (jnp.where(s[0] == core, i, 0), 0, part))

    each = pl.BlockSpec((z.g, B, half), lambda i, s: (i, 0, 0))
    pair = shape(blocks_here, B, KP, dtype=BF16)
    p_high, p_low, z_pair = pl.pallas_call(
        functools.partial(panel_kernel, z),
        out_shape=[pair, pair, shape(2, PW, PW, dtype=BF16)],
        grid_spec=pltpu.PrefetchScalarGridSpec(
            num_scalar_prefetch=1,
            grid=(z.tiles,),
            in_specs=[ANY] * 2 + [tile(KP, 1)],
            out_specs=[tile(KP, 1), tile(KP, 1), WHOLE],
            scratch_shapes=[
                pltpu.VMEM((z.g * B, KP), F32),
                pltpu.VMEM((fronts, EXT, KP), F32),
                pltpu.VMEM((PW, 2 * PW), F32),
                pltpu.SMEM((fronts,), jnp.int32),
                pltpu.SemaphoreType.DMA((NB + 1,)),
            ],
        ),
        compiler_params=PARAMS,
        cost_estimate=SHORT,
        name="panel_rows",
    )(info, mine, theirs, other)

    l1, i1 = pl.pallas_call(
        functools.partial(factor1_kernel, z),
        out_shape=[shape(PW, PW)] * 2,
        in_specs=[SCALARS] + [ANY] * (rows + 1),
        out_specs=[WHOLE] * 2,
        scratch_shapes=factor_scratch[:1]
        + [pltpu.VMEM((PW, 2 * PW), F32)]
        + factor_scratch[1:]
        + [pltpu.SemaphoreType.DMA((rows + NB,))],
        compiler_params=PARAMS,
        cost_estimate=SHORT,
        name="factor1",
    )(info, after(mine, p_low), *pivots)
    i1_other = to_other(i1)

    w_next, y0 = pl.pallas_call(
        functools.partial(window_solve_kernel, z),
        out_shape=[shape(half, PW), shape(2, half, PW, dtype=BF16)],
        in_specs=[SCALARS] + [ANY] * (2 + z.gathers),
        out_specs=[ANY, ANY],
        scratch_shapes=[
            pltpu.VMEM((half, KP), F32),
            pltpu.VMEM((PW, 2 * PW), F32),
            pltpu.VMEM((2, 2, PW, PW), BF16),
            pltpu.VMEM((2, half, PW), BF16),
            pltpu.SemaphoreType.DMA((rows * z.windows + NB + 3,)),
        ],
        compiler_params=PARAMS,
        cost_estimate=SHORT,
        name="window_solve",
    )(info, after(theirs, i1), z_pair, *windows)

    rest_rows = half - KP + -(-fronts * (half - KP) // KP) * B
    rest = pl.pallas_call(
        functools.partial(pick_kernel, z),
        out_shape=shape(rest_rows, KP),
        in_specs=[SCALARS] + [ANY] * (z.gathers + fronts),
        out_specs=ANY,
        scratch_shapes=[
            pltpu.VMEM((rest_rows, KP), F32),
            pltpu.SemaphoreType.DMA((rows * z.windows + fronts + 1,)),
        ],
        compiler_params=PARAMS,
        cost_estimate=SHORT,
        name="pick",
    )(info, *windows, *after(tuple(late), w_next))
    rest = from_other(rest)

    out = pl.pallas_call(
        functools.partial(final_kernel, z),
        out_shape=shape(blocks_here, B, half),
        grid_spec=pltpu.PrefetchScalarGridSpec(
            num_scalar_prefetch=1,
            grid=(z.tiles,),
            in_specs=[ANY] * (9 + fronts) + [each, tile(KP, 1), tile(KP, 1)],
            out_specs=each,
            scratch_shapes=[
                pltpu.VMEM((z.g * B, KP), F32),
                pltpu.VMEM((fronts, EXT, KP), F32),
                pltpu.VMEM((half // PW, PW, PW), F32),
                pltpu.VMEM((fronts, B, half), F32),
                pltpu.VMEM((PW, PW), F32),
                pltpu.VMEM((PW, 2 * PW), F32),
                pltpu.VMEM((5, 2, PW, PW), BF16),
                pltpu.VMEM((2, 2, half, PW), BF16),
                pltpu.SMEM((fronts,), jnp.int32),
                pltpu.SemaphoreType.DMA((2 * fronts + half // PW + NB + 4,)),
            ],
        ),
        compiler_params=PARAMS,
        cost_estimate=SHORT,
        name="final",
    )(info, mine, theirs, rest, i1, i1_other, l0, l1, w_next, y0, *late, matrix, p_high, p_low)
    return out[None]


def solution(mesh):
    return jax.shard_map(
        on_device,
        mesh=mesh,
        in_specs=(
            P("front", None, "row", "col"),
            P("front"),
            P("front", None, "row", "col"),
            P("front", None, "row"),
            P("front", None, "row"),
        ),
        out_specs=P("front", None, "row", "col"),
        check_vma=False,
    )
```

```python
import functools

import jax
import jax.numpy as jnp
from jax import lax
from jax.experimental import pallas as pl
from jax.experimental.pallas import tpu as pltpu
from jax.sharding import PartitionSpec as P

PW = 512
NPANEL = 2
B = 128
KP = PW * NPANEL
NB = PW // B
EXT = B + 8
NT = ((1,), (1,))
NN = ((1,), (0,))
TN = ((0,), (0,))
F32 = jnp.float32
BF16 = jnp.bfloat16
VMEM_LIMIT = 56 * 2**20


def split(x):
    high = x.astype(BF16)
    return high, (x - high.astype(F32)).astype(BF16)


def dot3(a, b, dims):
    def one(u, v):
        return lax.dot_general(u, v, (dims, ((), ())), preferred_element_type=F32)

    return one(a[0], b[0]) + (one(a[0], b[1]) + one(a[1], b[0]))


def dot6(a, b, dims):
    return lax.dot_general(
        a, b, (dims, ((), ())), precision=lax.Precision.HIGHEST, preferred_element_type=F32
    )


def over_lanes(group, lane):
    return jnp.broadcast_to(group[:, lane : lane + 1], group.shape)


def over_rows(group, row):
    return jnp.broadcast_to(group[row : row + 1, :], group.shape)


def factor_block(s_ref, v_ref, u_ref):
    sub = lax.broadcasted_iota(jnp.int32, (8, B), 0)
    lane = lax.broadcasted_iota(jnp.int32, (8, B), 1)
    n = B // 8
    left = [s_ref[8 * g : 8 * g + 8, :] for g in range(n)]
    right = [jnp.where(lane == sub + 8 * g, 1.0, 0.0).astype(F32) for g in range(n)]
    for b in range(n):
        cols = [[over_lanes(left[g], 8 * b + j) for j in range(8)] for g in range(b, n)]
        scale = jnp.ones((8, B), F32)
        for j in range(8):
            pivot = over_rows(cols[0][j], j)
            inv = 1.0 / pivot
            lrow = over_rows(left[b], j)
            rrow = over_rows(right[b], j)
            krow = [over_rows(cols[0][k], j) if k > j else None for k in range(8)]
            scale = jnp.where(sub == j, lax.rsqrt(pivot), scale)
            for g in range(b, n):
                f = cols[g - b][j] * inv
                if g == b:
                    f = jnp.where(sub > j, f, 0.0)
                for k in range(j + 1, 8):
                    cols[g - b][k] = cols[g - b][k] - f * krow[k]
                left[g] = left[g] - f * lrow
                right[g] = right[g] - f * rrow
        u_ref[8 * b : 8 * b + 8, :] = jnp.where(lane >= sub + 8 * b, left[b] * scale, 0.0)
        v_ref[8 * b : 8 * b + 8, :] = right[b] * scale


def panel_factor(m_ref, u_ref, v_ref):
    def body(k, _):
        c = pl.multiple_of(k * B, B)
        factor_block(m_ref.at[pl.ds(c, B), pl.ds(c, B)], v_ref, u_ref)
        row = dot6(v_ref[...], m_ref[pl.ds(c, B), :], NN)
        m_ref[pl.ds(c, B), :] = row
        m_ref[pl.ds(c, B), pl.ds(c, B)] = u_ref[...]
        for i in range(1, NB):

            @pl.when(i > k)
            def _():
                up = m_ref[pl.ds(c, B), i * B : (i + 1) * B]
                rows = slice(i * B, (i + 1) * B)
                m_ref[rows, :] = m_ref[rows, :] - dot6(up, row, TN)

        return 0

    lax.fori_loop(0, NB, body, 0)


def load_symmetric(a_ref, m_ref, col):
    r = lax.broadcasted_iota(jnp.int32, (B, B), 0)
    c = lax.broadcasted_iota(jnp.int32, (B, B), 1)
    for i in range(NB):
        for j in range(NB):
            here = (slice(i * B, (i + 1) * B), slice(PW + j * B, PW + (j + 1) * B))
            m_ref[here] = jnp.where(r == c, 1.0, 0.0) if i == j else jnp.zeros((B, B), F32)
            if j > i:
                continue
            block = a_ref[i * B : (i + 1) * B, col + j * B : col + (j + 1) * B]
            if i == j:
                block = jnp.where(r >= c, block, block.T)
                m_ref[i * B : (i + 1) * B, i * B : (i + 1) * B] = block
            else:
                m_ref[i * B : (i + 1) * B, j * B : (j + 1) * B] = block
                m_ref[j * B : (j + 1) * B, i * B : (i + 1) * B] = block.T


def store_factor(m_ref, l_ref, i_ref):
    for i in range(NB):
        for j in range(NB):
            here = (slice(i * B, (i + 1) * B), slice(j * B, (j + 1) * B))
            if j <= i:
                l_ref[here] = m_ref[j * B : (j + 1) * B, i * B : (i + 1) * B].T
            else:
                l_ref[here] = jnp.zeros((B, B), F32)
    i_ref[...] = m_ref[:, PW:]


class Copies:
    def __init__(self, sems):
        self.sems, self.count = sems, 0

    def start(self, src, dst, when=None):
        copy = pltpu.make_async_copy(src, dst, self.sems.at[self.count])
        self.count += 1
        if when is None:
            copy.start()
        else:
            pl.when(when)(copy.start)
        return copy, when

    @staticmethod
    def wait(started):
        for copy, when in started:
            if when is None:
                copy.wait()
            else:
                pl.when(when)(copy.wait)


def take_rows(copies, me, pieces, dst, first, count, pick, cols):
    started = []
    rows = len(pieces)
    for k, piece in enumerate(pieces):
        for l, src in pick(piece):
            at = (me ^ k) + l * rows - first
            low, high = l * rows - first, l * rows - first + rows - 1
            inside = None if low >= 0 and high < count else (at >= 0) & (at < count)
            clipped = at if inside is None else jnp.clip(at, 0, count - 1)
            here = pl.ds(pl.multiple_of(clipped * B, B), B)
            started.append(copies.start(src, dst.at[here, cols], inside))
    return started


class Sizes:
    def __init__(self, rows, fronts, per_device, blocks_here, half):
        self.rows, self.fronts, self.kb = rows, fronts, per_device
        self.blocks, self.half = blocks_here, half
        self.npl = KP // (rows * B)
        self.g = max(1, blocks_here // 6)
        self.tiles = blocks_here // self.g
        self.windows = 2 * half // (rows * B) - self.npl
        self.pivot_first = 0 if self.npl == 2 else NB
        self.pivot_cols = PW if self.npl == 2 else 0
        self.gathers = rows + 1 if rows == 4 and self.windows % 2 == 0 else rows
        self.a_first = KP // B
        self.a_count = (half - KP) // B
        self.b_first = half // B
        self.b_count = half // B

    def narrow_at(self, d):
        width = self.half - KP
        per = KP // width
        return (pl.ds(self.half - KP + d // per * B, B), pl.ds(d % per * width, width))

    def window_blocks(self, first, count):
        return range(first // self.rows - self.npl, (first + count - 1) // self.rows + 1 - self.npl)


def gathered(z, refs):
    if len(refs) == z.rows:
        return [lambda l, ref=ref: ref.at[l] for ref in refs]
    half = z.windows // 2
    whole, (first, second) = refs[: z.rows - 1], refs[z.rows - 1 :]
    across = lambda l: first.at[l] if l < half else second.at[l - half]
    return [lambda l, ref=ref: ref.at[l] for ref in whole] + [across]


def route(z, info, d):
    front = lax.rem(info[3] + d, z.fronts)
    slot, place = jnp.int32(0), jnp.int32(-1)
    for k in range(z.kb):
        hit = info[4 + k] == front
        slot = jnp.where(hit, k, slot)
        place = jnp.where(hit, info[4 + z.kb + k], place)
    return slot, place


def read_places(z, blocks, places, first=B):
    for d in range(z.fronts):
        places[d] = jnp.max(blocks[d, first : first + EXT - B, :B]).astype(jnp.int32)


def factor0_kernel(z, info, *refs):
    pieces, (l_out, i_out, a_ref, m_ref, u_ref, v_ref, sems) = refs[: z.rows], refs[z.rows :]

    @pl.when(info[0] == 0)
    def _():
        copies = Copies(sems)
        pick = lambda piece: [(0, piece.at[:, pl.ds(0, PW)])]
        copies.wait(take_rows(copies, info[1], pieces, a_ref, 0, NB, pick, slice(None)))
        load_symmetric(a_ref, m_ref, 0)
        panel_factor(m_ref, u_ref, v_ref)
        store_factor(m_ref, l_out, i_out)


def middle_kernel(z, info, i0_ref, *refs):
    pieces, (out, a_ref, f_s, sems) = refs[: z.rows], refs[z.rows :]

    @pl.when(info[0] == 0)
    def _():
        copies = Copies(sems)
        pick = lambda piece: [(0, piece.at[:, pl.ds(z.pivot_cols, PW)])]
        started = take_rows(copies, info[1], pieces, a_ref, z.pivot_first, NB, pick, slice(None))
        started.append(copies.start(i0_ref, f_s.at[:, pl.ds(0, PW)]))
        copies.wait(started)
        f_s[:, PW:] = dot6(a_ref[...], f_s[:, :PW], NT)
        copies.wait(
            [copies.start(f_s.at[pl.ds(n * B, B)], out.at[n, pl.ds(0, B)]) for n in range(NB)]
        )


def take_factor(copies, packed, f_s):
    return [copies.start(packed.at[n, pl.ds(0, B)], f_s.at[pl.ds(n * B, B)]) for n in range(NB)]


def sort_kernel(z, info, first, second, *refs):
    f = z.fronts
    panel, late = refs[:f], refs[f : 2 * f]
    c_s, e_s, sems = refs[2 * f :]
    narrow = z.half - KP

    @pl.when(info[0] == 1)
    def _():
        copies = Copies(sems)
        routes = [route(z, info, d) for d in range(f)]
        order = list(range(1, f)) + [0]
        reads = {}
        for d in order:
            slot, place = routes[d]
            c_s[d, B:EXT, :B] = jnp.full((EXT - B, B), place.astype(F32))
            reads[d] = copies.start(first.at[slot, :, pl.ds(0, KP)], c_s.at[d, pl.ds(0, B)])
        more = []
        for d in order:
            slot = routes[d][0]
            more.append(
                copies.start(first.at[slot, :, pl.ds(KP, narrow)], e_s.at[d, :, pl.ds(0, narrow)])
            )
            more.append(copies.start(second.at[slot], e_s.at[d, :, pl.ds(narrow, z.half)]))
        writes = []
        for d in order:
            copies.wait([reads[d]])
            writes.append(copies.start(c_s.at[d], panel[d]))
        for n, d in enumerate(order):
            copies.wait(more[2 * n : 2 * n + 2])
            writes.append(copies.start(e_s.at[d], late[d]))
        copies.wait(writes)


def window_kernel(z, info, raw, _, *refs):
    f = z.fronts
    panel, (window, back), (t_ref, c_ref, places, sems) = refs[:f], refs[f : f + 2], refs[f + 2 :]

    @pl.when(info[0] == 1)
    def _():
        copies = Copies(sems)
        started = [copies.start(raw, t_ref)]
        started += [copies.start(panel[d], c_ref.at[d]) for d in range(f)]
        copies.wait(started)
        later = [copies.start(c_ref, back)]
        read_places(z, c_ref, places)
        for d in range(f):
            place = places[d] - z.npl

            @pl.when((place >= 0) & (place < z.windows))
            def _():
                t_ref[place] += c_ref[d, :B]

        later.append(copies.start(t_ref, window))
        copies.wait(later)


def fill_panel(z, info, places, blocks, i, p_ref, t_ref):
    for l in range(z.g):
        lb = i * z.g + l
        valid = (lb * z.rows + info[1]) * B < info[2]
        t_ref[l * B : (l + 1) * B, :] = jnp.where(valid, p_ref[l, :, :KP], 0.0)
    for d in range(z.fronts):
        at = places[d] - i * z.g

        @pl.when((at >= 0) & (at < z.g))
        def _():
            here = pl.ds(pl.multiple_of(at * B, B), B)
            t_ref[here, :] += blocks[d, :B]


def factor1_kernel(z, info, mine, *refs):
    pieces, (l_out, i_out, a_ref, f_s, m_ref, u_ref, v_ref, sems) = refs[: z.rows], refs[z.rows :]

    @pl.when(info[0] == 0)
    def _():
        copies = Copies(sems)
        pick = lambda piece: [(0, piece.at[:, pl.ds(z.pivot_cols + PW, PW)])]
        started = take_rows(copies, info[1], pieces, a_ref, z.pivot_first, NB, pick, slice(None))
        started += take_factor(copies, mine, f_s)
        copies.wait(started)
        load_symmetric(a_ref, m_ref, 0)
        m_ref[:, :PW] = m_ref[:, :PW] - dot6(f_s[:, PW:], f_s[:, PW:], NT)
        panel_factor(m_ref, u_ref, v_ref)
        store_factor(m_ref, l_out, i_out)


def panel_kernel(z, info, mine, theirs, p_ref, p_high, p_low, z_out, t_s, c_s, f_s, places, sems):
    i = pl.program_id(0)

    @pl.when(info[0] == 1)
    def _():
        @pl.when(i == 0)
        def _():
            copies = Copies(sems)
            started = take_factor(copies, theirs, f_s)
            started.append(copies.start(mine, c_s))
            copies.wait(started)
            read_places(z, c_s, places)
            product = dot3(split(f_s[:, PW:]), split(f_s[:, :PW]), NN)
            z_out[0], z_out[1] = split(product)

        fill_panel(z, info, places, c_s, i, p_ref, t_s)
        p = split(t_s[:, :PW])
        later = split(t_s[:, PW:] - dot3(p, (z_out[0], z_out[1]), NT))
        for out, first, second in ((p_high, p[0], later[0]), (p_low, p[1], later[1])):
            out[:, :, :PW] = first.reshape(z.g, B, PW)
            out[:, :, PW:] = second.reshape(z.g, B, PW)


def each_chunk(z, body):
    def step(n, _):
        body(pl.ds(pl.multiple_of(n * PW, PW), PW))
        return 0

    lax.fori_loop(0, z.half // PW, step, 0)


def window_solve_kernel(z, info, theirs, z_ref, *refs):
    w, refs = gathered(z, refs[: z.gathers]), refs[z.gathers :]
    w_out, y_out, w_s, f_s, inv, y, sems = refs

    @pl.when(info[0] == 1)
    def _():
        copies = Copies(sems)
        used = z.window_blocks(z.b_first, z.b_count)
        pick = lambda piece: [(l + z.npl, piece(l)) for l in used]
        started = take_factor(copies, theirs, f_s)
        started.append(copies.start(z_ref, inv.at[1]))
        started += take_rows(copies, info[1], w, w_s, z.b_first, z.b_count, pick, slice(None))
        copies.wait(started)
        inv[0, 0], inv[0, 1] = split(f_s[:, :PW])

        base = copies.count

        def outgoing(n, span):
            return [
                pltpu.make_async_copy(y.at[:, span], y_out.at[:, span], sems.at[base + 2 * n]),
                pltpu.make_async_copy(w_s.at[span, pl.ds(PW, PW)], w_out.at[span], sems.at[base + 2 * n + 1]),
            ]

        def project(n, _):
            span = pl.ds(pl.multiple_of(n * PW, PW), PW)
            inverse = (inv[0, 0], inv[0, 1])
            first = split(w_s[span, :PW])
            x = split(dot3(first, inverse, NT))
            y[0, span, :], y[1, span, :] = split(dot3(x, inverse, NN))
            w_s[span, PW:] = w_s[span, PW:] - dot3(first, (inv[1, 0], inv[1, 1]), NT)
            for copy in outgoing(n, span):
                copy.start()
            return 0

        lax.fori_loop(0, z.half // PW, project, 0)
        for n in range(z.half // PW):
            for copy in outgoing(n, pl.ds(n * PW, PW)):
                copy.wait()


def pick_kernel(z, info, *refs):
    w, refs = gathered(z, refs[: z.gathers]), refs[z.gathers :]
    late, (out, w_s, sems) = refs[: z.fronts], refs[z.fronts :]
    narrow = z.half - KP

    @pl.when(info[0] == 1)
    def _():
        copies = Copies(sems)
        used = z.window_blocks(z.a_first, z.a_count)
        pick = lambda piece: [(l + z.npl, piece(l)) for l in used]
        started = take_rows(copies, info[1], w, w_s, z.a_first, z.a_count, pick, slice(None))
        for d in range(z.fronts):
            started.append(copies.start(late[d].at[:, pl.ds(0, narrow)], w_s.at[z.narrow_at(d)]))
        copies.wait(started)
        copies.wait([copies.start(w_s, out)])


def final_kernel(z, info, mine, theirs, rest, i1_ref, i1r_ref, l0_ref, l1_ref, w_ref, y_ref, *refs):
    f = z.fronts
    late, (x_ref, p_high, p_low, out), refs = refs[:f], refs[f : f + 4], refs[f + 4 :]
    t_s, c_s, w_s, e_s, i_s, s_s, inv, y, places, sems = refs
    i = pl.program_id(0)

    def add_late(cols):
        for d in range(f):
            at = places[d] - i * z.g

            @pl.when((at >= 0) & (at < z.g))
            def _():
                out[at, :, cols] += e_s[d, :, cols]

    def valid(l):
        return ((i * z.g + l) * z.rows + info[1]) * B < info[2]

    @pl.when(info[0] == 0)
    def _():
        copies = Copies(sems)

        @pl.when(i == 0)
        def _():
            started = [
                copies.start(rest.at[pl.ds(0, PW), pl.ds(0, PW)], w_s.at[0]),
                copies.start(rest.at[pl.ds(0, PW), pl.ds(PW, PW)], w_s.at[1]),
                copies.start(i1_ref, i_s),
                copies.start(theirs, c_s),
            ]
            started += take_factor(copies, mine, s_s)
            right = pl.ds(KP, z.half - KP)
            arriving = [copies.start(rest.at[z.narrow_at(d)], e_s.at[d, :, right]) for d in range(f)]
            copies.wait(started)
            read_places(z, c_s, places)
            for n, value in enumerate((s_s[:, :PW], s_s[:, PW:], i_s[...])):
                inv[n, 0], inv[n, 1] = split(value)
            x = split(dot3(split(w_s[0]), (inv[0, 0], inv[0, 1]), NT))
            inv[3, 0], inv[3, 1] = x
            later = split(w_s[1] - dot3(x, (inv[1, 0], inv[1, 1]), NT))
            inv[4, 0], inv[4, 1] = split(dot3(later, (inv[2, 0], inv[2, 1]), NT))
            copies.wait(arriving)

        fill_panel(z, info, places, c_s, i, x_ref, t_s)
        x0 = dot3(split(t_s[:, :PW]), (inv[0, 0], inv[0, 1]), NT)
        x0s = split(x0)
        later = split(t_s[:, PW:] - dot3(x0s, (inv[1, 0], inv[1, 1]), NT))
        x1 = dot3(later, (inv[2, 0], inv[2, 1]), NT)
        update = dot3(x0s, (inv[3, 0], inv[3, 1]), NT) + dot3(split(x1), (inv[4, 0], inv[4, 1]), NT)
        for l in range(z.g):
            span = slice(l * B, (l + 1) * B)
            out[l, :, :PW] = x0[span]
            out[l, :, PW:KP] = x1[span]
            out[l, :, KP:] = jnp.where(valid(l), x_ref[l, :, KP:], 0.0) - update[span]
        add_late(slice(KP, z.half))

        @pl.when(i == 0)
        def _():
            for l in range(z.npl):
                row = (l * z.rows + info[1]) * B
                out[l, :, PW:] = jnp.zeros((B, z.half - PW), F32)

                @pl.when(row < PW)
                def _():
                    here = pl.ds(pl.multiple_of(row, B), B)
                    copy = pltpu.make_async_copy(l0_ref.at[here], out.at[l, :, pl.ds(0, PW)], sems.at[0])
                    copy.start()
                    copy.wait()

                @pl.when(row >= PW)
                def _():
                    here = pl.ds(pl.multiple_of(row - PW, B), B)
                    out[l, :, :PW] = s_s[here, PW:]
                    copy = pltpu.make_async_copy(l1_ref.at[here], out.at[l, :, pl.ds(PW, PW)], sems.at[0])
                    copy.start()
                    copy.wait()

    @pl.when(info[0] == 1)
    def _():
        copies = Copies(sems)

        @pl.when(i == 0)
        def _():
            started = [
                copies.start(i1r_ref, i_s),
                copies.start(mine.at[:, pl.ds(B, EXT - B)], c_s.at[:, pl.ds(B, EXT - B)]),
            ]
            for n in range(z.half // PW):
                started.append(copies.start(w_ref.at[pl.ds(n * PW, PW)], w_s.at[n]))
            arriving = [copies.start(y_ref, y.at[0])]
            right = pl.ds(z.half - KP, z.half)
            arriving += [copies.start(late[d].at[:, right], e_s.at[d]) for d in range(f)]
            copies.wait(started)
            read_places(z, c_s, places)
            inverse = split(i_s[...])
            inv[0, 0], inv[0, 1] = inverse

            def project(n, _):
                inverse = (inv[0, 0], inv[0, 1])
                span = pl.ds(pl.multiple_of(n * PW, PW), PW)
                x = split(dot3(split(w_s[n]), inverse, NT))
                y[1, 0, span, :], y[1, 1, span, :] = split(dot3(x, inverse, NN))
                return 0

            lax.fori_loop(0, z.half // PW, project, 0)
            copies.wait(arriving)

        p0 = tuple(p[:, :, :PW].reshape(z.g * B, PW) for p in (p_high, p_low))
        p1 = tuple(p[:, :, PW:].reshape(z.g * B, PW) for p in (p_high, p_low))

        def subtract(span):
            update = dot3(p0, (y[0, 0, span, :], y[0, 1, span, :]), NT)
            update = update + dot3(p1, (y[1, 0, span, :], y[1, 1, span, :]), NT)
            for l in range(z.g):
                present = jnp.where(valid(l), x_ref[l, :, span], 0.0)
                out[l, :, span] = present - update[l * B : (l + 1) * B]

        for n in range(z.half // PW):
            subtract(slice(n * PW, (n + 1) * PW))
        add_late(slice(0, z.half))

        @pl.when(i == 0)
        def _():
            for l in range(z.npl):
                out[l] = jnp.zeros((B, z.half), F32)


ANY = pl.BlockSpec(memory_space=pl.ANY)
WHOLE = pl.BlockSpec(memory_space=pltpu.VMEM)
SCALARS = pl.BlockSpec(memory_space=pltpu.SMEM)
PARAMS = pltpu.CompilerParams(vmem_limit_bytes=VMEM_LIMIT)
SHORT = pl.CostEstimate(flops=1, bytes_accessed=1, transcendentals=0)


def shape(*dims, dtype=F32):
    return jax.ShapeDtypeStruct(dims, dtype)


def after(value, *others):
    return lax.optimization_barrier((value, *others))[0]


def on_device(front_matrix, front_sizes, contrib, dest_front, dest_local):
    fronts = lax.axis_size("front")
    rows = lax.axis_size("row")
    front_here = lax.axis_index("front")
    row_here = lax.axis_index("row")
    col_here = lax.axis_index("col")
    matrix = front_matrix[0]
    blocks = contrib[0]
    blocks_here, _, half = matrix.shape
    z = Sizes(rows, fronts, blocks.shape[0], blocks_here, half)

    def from_rows(x, core):
        return [x] + [along_rows(x, k, core) for k in range(1, rows)]

    def along_rows(x, k, core):
        pairs = [(r * 2 + core, (r ^ k) * 2 + core) for r in range(rows)]
        return lax.ppermute(x, ("row", "col"), pairs)

    def along_fronts(x, d, source, target):
        pairs = [(f * 2 + source, (f + d) % fronts * 2 + target) for f in range(fronts)]
        return lax.ppermute(x, ("front", "col"), pairs)

    def to_other(x):
        return lax.ppermute(x, "col", [(0, 1)])

    def swap(x):
        return lax.ppermute(x, "col", [(0, 1), (1, 0)])

    def from_other(x):
        return lax.ppermute(x, "col", [(1, 0)])

    info = jnp.concatenate(
        [
            jnp.stack([col_here, row_here]).astype(jnp.int32),
            front_sizes,
            front_here.astype(jnp.int32)[None],
            dest_front[0, :, 0],
            dest_local[0, :, 0],
        ]
    )
    other_blocks = to_other(blocks)
    pivot = matrix[z.npl - 1, :, :KP]
    if z.npl == 2:
        pivot = jnp.concatenate([matrix[0, :, :PW], pivot], axis=1)
    pivots = from_rows(pivot, 0)
    raw = to_other(after(matrix, pivot)[z.npl : z.npl + z.windows, :, :KP])
    other = to_other(after(matrix, other_blocks, *pivots, raw))

    factor_scratch = [
        pltpu.VMEM((PW, PW), F32),
        pltpu.VMEM((PW, 2 * PW), F32),
        pltpu.VMEM((B, B), F32),
        pltpu.VMEM((B, B), F32),
    ]
    l0, i0 = pl.pallas_call(
        functools.partial(factor0_kernel, z),
        out_shape=[shape(PW, PW)] * 2,
        in_specs=[SCALARS] + [ANY] * rows,
        out_specs=[WHOLE] * 2,
        scratch_shapes=factor_scratch + [pltpu.SemaphoreType.DMA((rows,))],
        compiler_params=PARAMS,
        cost_estimate=SHORT,
        name="factor0",
    )(info, *pivots)
    packed = pl.pallas_call(
        functools.partial(middle_kernel, z),
        out_shape=shape(fronts, EXT, KP),
        in_specs=[SCALARS] + [ANY] * (rows + 1),
        out_specs=ANY,
        scratch_shapes=[
            pltpu.VMEM((PW, PW), F32),
            pltpu.VMEM((PW, 2 * PW), F32),
            pltpu.SemaphoreType.DMA((rows + NB + 1,)),
        ],
        compiler_params=PARAMS,
        cost_estimate=SHORT,
        name="middle",
    )(info, i0, *pivots)

    refs = pl.pallas_call(
        functools.partial(sort_kernel, z),
        out_shape=[shape(EXT, KP)] * fronts + [shape(B, 2 * half - KP)] * fronts,
        in_specs=[SCALARS] + [ANY] * 2,
        out_specs=[ANY] * (2 * fronts),
        scratch_shapes=[
            pltpu.VMEM((fronts, EXT, KP), F32),
            pltpu.VMEM((fronts, B, 2 * half - KP), F32),
            pltpu.SemaphoreType.DMA((5 * fronts,)),
        ],
        compiler_params=PARAMS,
        cost_estimate=SHORT,
        name="sort",
    )(info, other_blocks, blocks)
    panel, late = list(refs[:fronts]), list(refs[fronts:])
    panel = panel[:1] + [along_fronts(x, d + 1, 1, 1) for d, x in enumerate(panel[1:])]
    window, mine = pl.pallas_call(
        functools.partial(window_kernel, z),
        out_shape=[shape(z.windows, B, KP), shape(fronts, EXT, KP)],
        in_specs=[SCALARS] + [ANY] * (fronts + 2),
        out_specs=[ANY] * 2,
        input_output_aliases={2: 1},
        scratch_shapes=[
            pltpu.VMEM((z.windows, B, KP), F32),
            pltpu.VMEM((fronts, EXT, KP), F32),
            pltpu.SMEM((fronts,), jnp.int32),
            pltpu.SemaphoreType.DMA((fronts + 4,)),
        ],
        compiler_params=PARAMS,
        cost_estimate=SHORT,
        name="window",
    )(info, raw, packed, *panel)
    late = late[:1] + [along_fronts(after(x, window), d + 1, 1, 1) for d, x in enumerate(late[1:])]
    if z.gathers == rows:
        windows = from_rows(window, 1)
        theirs = swap(mine)
    else:
        middle = z.windows // 2
        sides = [along_rows(window, 1, 1), along_rows(window, 2, 1)]
        windows = [window, *sides]
        theirs = swap(after(mine, *sides, late[1], late[-1]))
        windows += [along_rows(sides[0][:middle], 2, 1), along_rows(sides[1][middle:], 1, 1)]

    def tile(width, core, part=0):
        return pl.BlockSpec((z.g, B, width), lambda i, s: (jnp.where(s[0] == core, i, 0), 0, part))

    each = pl.BlockSpec((z.g, B, half), lambda i, s: (i, 0, 0))
    pair = shape(blocks_here, B, KP, dtype=BF16)
    p_high, p_low, z_pair = pl.pallas_call(
        functools.partial(panel_kernel, z),
        out_shape=[pair, pair, shape(2, PW, PW, dtype=BF16)],
        grid_spec=pltpu.PrefetchScalarGridSpec(
            num_scalar_prefetch=1,
            grid=(z.tiles,),
            in_specs=[ANY] * 2 + [tile(KP, 1)],
            out_specs=[tile(KP, 1), tile(KP, 1), WHOLE],
            scratch_shapes=[
                pltpu.VMEM((z.g * B, KP), F32),
                pltpu.VMEM((fronts, EXT, KP), F32),
                pltpu.VMEM((PW, 2 * PW), F32),
                pltpu.SMEM((fronts,), jnp.int32),
                pltpu.SemaphoreType.DMA((NB + 1,)),
            ],
        ),
        compiler_params=PARAMS,
        cost_estimate=SHORT,
        name="panel_rows",
    )(info, mine, theirs, other)

    l1, i1 = pl.pallas_call(
        functools.partial(factor1_kernel, z),
        out_shape=[shape(PW, PW)] * 2,
        in_specs=[SCALARS] + [ANY] * (rows + 1),
        out_specs=[WHOLE] * 2,
        scratch_shapes=factor_scratch[:1]
        + [pltpu.VMEM((PW, 2 * PW), F32)]
        + factor_scratch[1:]
        + [pltpu.SemaphoreType.DMA((rows + NB,))],
        compiler_params=PARAMS,
        cost_estimate=SHORT,
        name="factor1",
    )(info, after(mine, p_low), *pivots)
    i1_other = to_other(i1)

    w_next, y0 = pl.pallas_call(
        functools.partial(window_solve_kernel, z),
        out_shape=[shape(half, PW), shape(2, half, PW, dtype=BF16)],
        in_specs=[SCALARS] + [ANY] * (2 + z.gathers),
        out_specs=[ANY, ANY],
        scratch_shapes=[
            pltpu.VMEM((half, KP), F32),
            pltpu.VMEM((PW, 2 * PW), F32),
            pltpu.VMEM((2, 2, PW, PW), BF16),
            pltpu.VMEM((2, half, PW), BF16),
            pltpu.SemaphoreType.DMA((rows * z.windows + NB + 2 * half // PW + 1,)),
        ],
        compiler_params=PARAMS,
        cost_estimate=SHORT,
        name="window_solve",
    )(info, after(theirs, i1), z_pair, *windows)

    rest_rows = half - KP + -(-fronts * (half - KP) // KP) * B
    rest = pl.pallas_call(
        functools.partial(pick_kernel, z),
        out_shape=shape(rest_rows, KP),
        in_specs=[SCALARS] + [ANY] * (z.gathers + fronts),
        out_specs=ANY,
        scratch_shapes=[
            pltpu.VMEM((rest_rows, KP), F32),
            pltpu.SemaphoreType.DMA((rows * z.windows + fronts + 1,)),
        ],
        compiler_params=PARAMS,
        cost_estimate=SHORT,
        name="pick",
    )(info, *windows, *after(tuple(late), w_next))
    rest = from_other(rest)

    out = pl.pallas_call(
        functools.partial(final_kernel, z),
        out_shape=shape(blocks_here, B, half),
        grid_spec=pltpu.PrefetchScalarGridSpec(
            num_scalar_prefetch=1,
            grid=(z.tiles,),
            in_specs=[ANY] * (9 + fronts) + [each, tile(KP, 1), tile(KP, 1)],
            out_specs=each,
            scratch_shapes=[
                pltpu.VMEM((z.g * B, KP), F32),
                pltpu.VMEM((fronts, EXT, KP), F32),
                pltpu.VMEM((half // PW, PW, PW), F32),
                pltpu.VMEM((fronts, B, half), F32),
                pltpu.VMEM((PW, PW), F32),
                pltpu.VMEM((PW, 2 * PW), F32),
                pltpu.VMEM((5, 2, PW, PW), BF16),
                pltpu.VMEM((2, 2, half, PW), BF16),
                pltpu.SMEM((fronts,), jnp.int32),
                pltpu.SemaphoreType.DMA((2 * fronts + half // PW + NB + 4,)),
            ],
        ),
        compiler_params=PARAMS,
        cost_estimate=SHORT,
        name="final",
    )(info, mine, theirs, rest, i1, i1_other, l0, l1, w_next, y0, *late, matrix, p_high, p_low)
    return out[None]


def solution(mesh):
    return jax.shard_map(
        on_device,
        mesh=mesh,
        in_specs=(
            P("front", None, "row", "col"),
            P("front"),
            P("front", None, "row", "col"),
            P("front", None, "row"),
            P("front", None, "row"),
        ),
        out_specs=P("front", None, "row", "col"),
        check_vma=False,
    )
```
